512 devices in a mesh: row: 32 (over x, z_hi, core), col: 16 (over y, z_lo).
Axes of the slice: x: 4, y: 4, z: 16 (z_hi: 4, z_lo: 4; z = z_hi * 4 + z_lo), core: 2. Of those that a mesh axis runs over, the one named last changes fastest.
Arguments:
- x_block: bfloat16 [8, 131072], P(None, ('row', 'col')), may hold values from -6 to 6
- p_block: bfloat16 [8, 131072], P(None, ('row', 'col')), may hold values from -6 to 6
- tile_values: bfloat16 [24576, 128, 128], P(('row', 'col')), may hold values from -0.109375 to 0.109375
- tile_brow: int32 [24576], P(('row', 'col')), may hold values from 0 to 1023, as said below
- tile_bcol: int32 [24576], P(('row', 'col')), may hold values from 0 to 1023, as said below
- tile_count: int32 [512], P(('row', 'col')), may hold values from 1 to 48, as said below
Outputs:
- images: float32 [16, 131072], P(None, ('row', 'col'))
- projected: float32 [2, 16, 16], replicated
The draws below stay inside these ranges and needn't reach their ends.
Inputs may be any that keep to these rules, and one draw needn't show every extreme that they name: Slot k belongs to device d = k // 48 with grid row r = d // 16 and column c = d % 16; tile_brow[k] // 2 lies in r * 16 to r * 16 + 15, and tile_bcol[k] <= tile_brow[k]. Repeated tiles add. tile_bcol[k] // 2 = c + 16 * m for some m, with c the column of the slot's device as above. `tile_count`: every device of the last grid row has 48 live slots.
All inputs are finite; a program needn't handle non-finite values.
Results may differ from the reference program's by a relative error of at most 0.0003.
Values may be sent and summed in bfloat16 or wider, within the bound.
A program may use at most 64 MiB of HBM per device.

```python
import jax
import jax.numpy as jnp
from jax import lax

TB = 128
VECS = 8
CB = 2
TILES_DEV = 48
ROW_GROUPS = 32
COL_GROUPS = 16
NB = 1024
NDIM = 131072
TILES = 24576
DEVICES = 512


def tile_pattern(key):
    slots = jnp.arange(TILES) // TILES_DEV
    grid_row = slots // COL_GROUPS
    grid_col = slots % COL_GROUPS
    keys = jax.random.split(key, 4)
    chosen = jax.random.randint(keys[0], (TILES,), 0, grid_row + 1)
    inner = jax.random.randint(keys[1], (TILES,), 0, COL_GROUPS)
    inner = jnp.where(chosen == grid_row, grid_col + inner % (COL_GROUPS - grid_col), inner)
    row_off = jax.random.randint(keys[2], (TILES,), 0, CB)
    col_off = jax.random.randint(keys[3], (TILES,), 0, CB)
    brow = (grid_row * COL_GROUPS + inner) * CB + row_off
    bcol = (grid_col + COL_GROUPS * chosen) * CB + col_off
    brow = jnp.maximum(brow, bcol)
    return (brow.astype(jnp.int32), bcol.astype(jnp.int32))


def draw_tile_brow(key, part):
    brow, bcol = tile_pattern(key)
    return brow


def draw_tile_bcol(key, part):
    brow, bcol = tile_pattern(key)
    return bcol


def draw_tile_count(key, part):
    key = jax.random.fold_in(key, 7)
    grid_row = jnp.arange(DEVICES) // COL_GROUPS
    base = TILES_DEV * (grid_row + 1) // ROW_GROUPS
    lowest = jnp.maximum(1, base // 2)
    highest = jnp.minimum(jnp.maximum(2, base), TILES_DEV)
    drawn = jax.random.randint(key, (DEVICES,), lowest, highest + 1)
    counts = jnp.where(grid_row == ROW_GROUPS - 1, TILES_DEV, drawn)
    return jnp.clip(counts, 1, TILES_DEV).astype(jnp.int32)


def block_scale(rng, dims, cuts, smallest, largest):
    loudness, own = 1.0, jax.random.fold_in(rng, 6)
    for dim, blocks in cuts:
        heights = jnp.exp(jax.random.uniform(jax.random.fold_in(own, dim), (blocks,), jnp.float32, smallest / len(cuts), largest / len(cuts)))
        loudness = loudness * jnp.repeat(heights, dims[dim] // blocks).reshape([-1 if axis == dim else 1 for axis in range(len(dims))])
    return loudness


def centred(own_key, extent, deviation, limit, shards=(), held_as=jnp.bfloat16):
    values = deviation * jax.random.normal(own_key, extent, jnp.float32)
    if shards:
        values = values * block_scale(own_key, extent, shards, -0.22, 0.18)
    return jnp.clip(values, -limit, limit).astype(held_as)


def setup_inputs(seed: int = 0) -> dict:
    splits = jax.random.split(jax.random.key(seed), 7)
    return {
        "x_block": centred(splits[0], (VECS, NDIM), 1.0, 6.0, ((1, 512),)),
        "p_block": centred(splits[1], (VECS, NDIM), 1.0, 6.0, ((1, 512),)),
        "tile_values": centred(splits[2], (TILES, TB, TB), (TB * TILES_DEV // CB) ** -0.5, 0.109375, ((0, 512),)),
        "tile_brow": draw_tile_brow(jax.random.fold_in(splits[6], 71), 0),
        "tile_bcol": draw_tile_bcol(jax.random.fold_in(splits[6], 71), 0),
        "tile_count": draw_tile_count(jax.random.fold_in(splits[6], 71), 0),
    }


def reference(x_block, p_block, tile_values, tile_brow, tile_bcol, tile_count):
    stacked = jnp.concatenate([x_block, p_block], axis=0)
    width = stacked.shape[0]
    blocked = stacked.reshape(width, NB, TB)
    live = (jnp.arange(TILES_DEV)[None, :] < tile_count[:, None]).astype(jnp.float32)
    values = tile_values.reshape(DEVICES, TILES_DEV, TB, TB)
    brows = tile_brow.reshape(DEVICES, TILES_DEV).astype(jnp.int32)
    bcols = tile_bcol.reshape(DEVICES, TILES_DEV).astype(jnp.int32)

    def step(total, item):
        tiles, brow, bcol, mask = item
        tiles = tiles.astype(jnp.float32)
        far = blocked[:, bcol].astype(jnp.float32)
        near = blocked[:, brow].astype(jnp.float32)
        down = jnp.einsum("kij,vkj->vki", tiles, far, precision=lax.Precision.HIGHEST) * mask[None, :, None]
        across = jnp.einsum("kij,vki->vkj", tiles, near, precision=lax.Precision.HIGHEST) * mask[None, :, None]
        total = total.at[:, brow].add(down)
        total = total.at[:, bcol].add(across)
        return total, None

    total, _ = lax.scan(step, jnp.zeros((width, NB, TB), jnp.float32), (values, brows, bcols, live))
    images = total.reshape(width, NDIM)
    floats = stacked.astype(jnp.float32)
    hamilton = jnp.dot(floats, images.T, precision=lax.Precision.HIGHEST) / NDIM
    correlation = jnp.dot(stacked, stacked.T, preferred_element_type=jnp.float32) / NDIM
    return images, jnp.stack([hamilton, correlation])
```

```python
import functools

import jax
import jax.numpy as jnp
from jax import lax
from jax.experimental import pallas as pl
from jax.experimental.pallas import tpu as pltpu
from jax.sharding import PartitionSpec as P

MESH = pl.DeviceIdType.MESH
F32 = jnp.float32
BF16 = jnp.bfloat16
VB = 16
TL = 128
NT = (((1,), (1,)), ((), ()))
NN = (((1,), (0,)), ((), ()))


def iota(shape, dim):
    return lax.broadcasted_iota(jnp.int32, shape, dim)


def split_dot(value, dims, other):
    return lax.dot_general(
        value, other, dims, precision=lax.Precision.HIGHEST, preferred_element_type=F32
    )


def fold_small(small):
    spread = (iota((VB, TL), 1) % VB == iota((VB, TL), 0)).astype(F32)
    wide = split_dot(small, NN, spread)
    keep = iota((VB, TL), 1) // VB == iota((VB, TL), 0) % 8
    wide = jnp.where(keep, wide, 0.0)
    top = jnp.sum(wide[0:8], axis=0, keepdims=True)
    low = jnp.sum(wide[8:16], axis=0, keepdims=True)
    return top, low


def unfold_small(top, low):
    keep = iota((VB, TL), 1) // VB == iota((VB, TL), 0) % 8
    upper = iota((VB, TL), 0) < 8
    wide = jnp.where(upper, jnp.broadcast_to(top, (VB, TL)), jnp.broadcast_to(low, (VB, TL)))
    wide = jnp.where(keep, wide, 0.0)
    gather = (iota((TL, VB), 0) % VB == iota((TL, VB), 1)).astype(F32)
    return split_dot(wide, NN, gather)


def kernel(
    slots,
    x_ref,
    p_ref,
    tiles_hbm,
    brow_s,
    bcol_s,
    brow_v,
    bcol_v,
    count_s,
    images_ref,
    small_ref,
    tiles,
    near,
    far,
    kron_row,
    kron_col,
    pieces,
    down_rows,
    across_rows,
    core_in,
    x_in,
    zh_in,
    y_in,
    zl_in,
    gram,
    z_small,
    xy_small,
    core_small,
    tile_sem,
    s_near,
    r_near,
    s_far,
    r_far,
    s_row,
    r_row,
    s_col,
    r_col,
    s_small,
    r_small,
):
    row, col = lax.axis_index("row"), lax.axis_index("col")
    x, zh, core = row // 8, (row // 2) % 4, row % 2
    y, zl = col // 4, col % 4

    def peer(dx=0, dy=0, dzh=0, dzl=0, dc=0):
        return (
            ((x + dx) % 4) * 8 + ((zh + dzh) % 4) * 2 + (core + dc) % 2,
            ((y + dy) % 4) * 4 + (zl + dzl) % 4,
        )

    def copy(src, dst, send, recv, to):
        return pltpu.make_async_remote_copy(
            src_ref=src, dst_ref=dst, send_sem=send, recv_sem=recv, device_id=to, device_id_type=MESH
        )

    def start(src, dst, send, recv, to):
        desc = copy(src, dst, send, recv, to)
        desc.start()
        return desc

    load = pltpu.make_async_copy(tiles_hbm, tiles, tile_sem)
    load.start()
    barrier = pltpu.get_barrier_semaphore()
    friends = (
        [peer(dzl=i) for i in (1, 2, 3)]
        + [peer(dy=i) for i in (1, 2, 3)]
        + [peer(dx=i) for i in (1, 2, 3)]
        + [peer(dzh=1), peer(dzh=3), peer(dc=1)]
    )
    for to in friends:
        pl.semaphore_signal(barrier, inc=1, device_id=to, device_id_type=MESH)

    for b in range(2):
        own = jnp.concatenate(
            [x_ref[:, b * TL : (b + 1) * TL].astype(F32), p_ref[:, b * TL : (b + 1) * TL].astype(F32)],
            axis=0,
        ).astype(BF16)
        near[b] = own
        far[b] = own

    def place(rel):
        lane = iota((8, slots), 1)
        rel = jnp.where(lane < count_s[0], jnp.broadcast_to(rel, (8, slots)), 255)
        spread = (iota((slots, slots * VB), 1) // VB == iota((slots, slots * VB), 0)).astype(BF16)
        wide = lax.dot_general(rel.astype(F32).astype(BF16), spread, NN, preferred_element_type=F32)
        wide = jnp.concatenate([wide, wide], axis=0)
        diag = iota((VB, slots * VB), 1) % VB == iota((VB, slots * VB), 0)
        return jnp.where(diag, wide, 255.0)

    def near_index(brow):
        c = (brow // 2) % 16
        return (((c // 4 - y) & 3) * 4 + ((c % 4 - zl) & 3)) * 2 + brow % 2

    def far_index(bcol):
        m = bcol // 32
        return (
            ((((m % 2) ^ core) * 4 + ((m // 8 - x) & 3)) * 4 + (((m // 2) % 4 - zh) & 3)) * 2 + bcol % 2
        )

    place_row = place(near_index(brow_v[...]))
    place_col = place(far_index(bcol_v[...]))

    def build(ref, placed, b):
        ref[pl.ds(pl.multiple_of(b * VB, VB), VB), :] = jnp.where(
            placed == b.astype(F32), 1.0, 0.0
        ).astype(BF16)

    @pl.loop(0, 64)
    def _(b):
        build(kron_col, place_col, b)

    @pl.loop(0, 32)
    def _(b):
        build(kron_row, place_row, b)

    pl.semaphore_wait(barrier, len(friends))
    sent = []

    near_zl = []
    for i in (3, 2, 1):
        near_zl.append(
            start(near.at[pl.ds(0, 2)], near.at[pl.ds((4 - i) * 2, 2)], s_near.at[i], r_near.at[i], peer(dzl=i))
        )
    far_up = start(far.at[pl.ds(0, 2)], far.at[pl.ds(6, 2)], s_far.at[0], r_far.at[0], peer(dzh=1))
    far_dn = start(far.at[pl.ds(0, 2)], far.at[pl.ds(2, 2)], s_far.at[1], r_far.at[1], peer(dzh=3))
    sent += near_zl + [far_up, far_dn]
    for d in near_zl:
        d.wait_recv()
    near_y = []
    for i in (2, 1, 3):
        near_y.append(
            start(
                near.at[pl.ds(0, 8)], near.at[pl.ds((4 - i) * 8, 8)], s_near.at[3 + i], r_near.at[3 + i], peer(dy=i)
            )
        )
    sent += near_y
    far_up.wait_recv()
    far_two = start(far.at[pl.ds(6, 2)], far.at[pl.ds(4, 2)], s_far.at[2], r_far.at[2], peer(dzh=1))
    far_dn.wait_recv()
    sent.append(far_two)
    for d in near_y:
        d.wait_recv()
    load.wait()

    def multiply(vec_ref, index_of, index_s, dims):
        @pl.loop(0, slots // 8)
        def _(step):
            for j in range(8):
                k = step * 8 + j
                vec = vec_ref[index_of(index_s[k])]
                part = lax.dot_general(vec, tiles[k], dims, preferred_element_type=F32)
                high = part.astype(BF16)
                rows = pl.ds(pl.multiple_of(k * VB, VB), VB)
                pieces[rows, 0:TL] = high
                pieces[rows, TL : 2 * TL] = (part - high.astype(F32)).astype(BF16)

    def scatter(kron, first, blocks, out_ref):
        both = lax.dot_general(
            kron[first * VB : (first + blocks) * VB, :], pieces[...], NN, preferred_element_type=F32
        )
        out_ref[first : first + blocks] = (both[:, 0:TL] + both[:, TL : 2 * TL]).reshape(blocks, VB, TL)

    multiply(near, near_index, brow_s, NN)
    for part in range(4):
        scatter(kron_col, 32 + part * 8, 8, across_rows)
    core_rs = start(across_rows.at[pl.ds(32, 32)], core_in, s_row.at[0], r_row.at[0], peer(dc=1))
    for part in range(4):
        scatter(kron_col, part * 8, 8, across_rows)
    far_two.wait_recv()
    far_x = []
    for i in (2, 1, 3):
        far_x.append(
            start(far.at[pl.ds(0, 8)], far.at[pl.ds((4 - i) * 8, 8)], s_far.at[2 + i], r_far.at[2 + i], peer(dx=i))
        )
    core_rs.wait_recv()
    x_rs = []
    for i in (2, 1, 3):
        across_rows[i * 8 : i * 8 + 8] += core_in[i * 8 : i * 8 + 8]
        x_rs.append(
            start(across_rows.at[pl.ds(i * 8, 8)], x_in.at[pl.ds((i - 1) * 8, 8)], s_row.at[i], r_row.at[i], peer(dx=i))
        )
    across_rows[0:8] += core_in[0:8]
    sent += [core_rs] + far_x + x_rs

    for d in far_x:
        d.wait_recv()
    far_core = start(far.at[pl.ds(0, 32)], far.at[pl.ds(32, 32)], s_far.at[6], r_far.at[6], peer(dc=1))
    sent.append(far_core)

    def hamilton_step(b, total):
        rows = across_rows[b]
        high = rows.astype(BF16)
        low = (rows - high.astype(F32)).astype(BF16)
        return (
            total
            + lax.dot_general(high, far[b], NT, preferred_element_type=F32)
            + lax.dot_general(low, far[b], NT, preferred_element_type=F32)
        )

    half = lax.fori_loop(0, 32, hamilton_step, jnp.zeros((VB, VB), F32), unroll=4)
    correlation = lax.dot_general(near[0], near[0], NT, preferred_element_type=F32) + lax.dot_general(
        near[1], near[1], NT, preferred_element_type=F32
    )
    h_top, h_low = fold_small(half)
    c_top, c_low = fold_small(correlation)
    gram[0, 0:1] = h_top
    gram[0, 1:2] = h_low
    gram[0, 2:3] = c_top
    gram[0, 3:4] = c_low
    small_z = []
    for n in range(1, 16):
        zz = zh * 4 + zl + n
        to = (x * 8 + ((zz // 4) % 4) * 2 + core, y * 4 + zz % 4)
        small_z.append(start(gram.at[0], z_small.at[n - 1], s_small.at[n - 1], r_small.at[n - 1], to))
    sent += small_z

    far_core.wait_recv()
    multiply(far, far_index, bcol_s, NT)
    y_rs = []
    for i in (2, 1, 3, 0):
        scatter(kron_row, i * 8, 8, down_rows)
        if i:
            y_rs.append(
                start(
                    down_rows.at[pl.ds(i * 8, 8)], y_in.at[pl.ds((i - 1) * 8, 8)], s_col.at[i], r_col.at[i], peer(dy=i)
                )
            )
    sent += y_rs

    for d in x_rs:
        d.wait_recv()
    zh_rs = []
    for i in (2, 1, 3, 0):
        mine = pl.ds(i * 2, 2)
        across_rows[mine] += x_in[i * 2 : i * 2 + 2] + x_in[8 + i * 2 : 10 + i * 2] + x_in[16 + i * 2 : 18 + i * 2]
        if i:
            zh_rs.append(
                start(across_rows.at[mine], zh_in.at[pl.ds((i - 1) * 2, 2)], s_row.at[3 + i], r_row.at[3 + i], peer(dzh=i))
            )
    sent += zh_rs

    for d in y_rs:
        d.wait_recv()
    zl_rs = []
    for i in (3, 2, 1, 0):
        mine = pl.ds(i * 2, 2)
        down_rows[mine] += y_in[i * 2 : i * 2 + 2] + y_in[8 + i * 2 : 10 + i * 2] + y_in[16 + i * 2 : 18 + i * 2]
        if i:
            zl_rs.append(
                start(down_rows.at[mine], zl_in.at[pl.ds((i - 1) * 2, 2)], s_col.at[3 + i], r_col.at[3 + i], peer(dzl=i))
            )
    sent += zl_rs

    for d in small_z:
        d.wait_recv()
    gram[1] = gram[0] + jnp.sum(z_small[...], axis=0)
    small_xy = []
    for n in range(1, 16):
        to = peer(dx=n // 4, dy=n % 4)
        small_xy.append(start(gram.at[1], xy_small.at[n - 1], s_small.at[14 + n], r_small.at[14 + n], to))
    sent += small_xy

    for d in zl_rs + zh_rs:
        d.wait_recv()
    for b in range(2):
        images_ref[:, b * TL : (b + 1) * TL] = (
            (down_rows[b] + across_rows[b])
            + ((zl_in[b] + zl_in[2 + b] + zl_in[4 + b]) + (zh_in[b] + zh_in[2 + b] + zh_in[4 + b]))
        )

    for d in small_xy:
        d.wait_recv()
    gram[2] = gram[1] + jnp.sum(xy_small[...], axis=0)
    small_core = start(gram.at[2], core_small, s_small.at[30], r_small.at[30], peer(dc=1))
    sent.append(small_core)
    small_core.wait_recv()
    scale = 1.0 / (512 * 256)
    whole = (gram[2] + core_small[...]) * scale
    part = unfold_small(whole[0:1], whole[1:2])
    eye = (iota((VB, VB), 0) == iota((VB, VB), 1)).astype(F32)
    small_ref[0] = part + lax.dot_general(
        eye, part, NT, precision=lax.Precision.HIGHEST, preferred_element_type=F32
    )
    small_ref[1] = unfold_small(whole[2:3], whole[3:4])
    for d in sent:
        d.wait_send()


def on_device(x_block, p_block, tile_values, tile_brow, tile_bcol, tile_count):
    slots = tile_values.shape[0]
    vmem = pl.BlockSpec(memory_space=pltpu.VMEM)
    smem = pl.BlockSpec(memory_space=pltpu.SMEM)
    dma = pltpu.SemaphoreType.DMA
    return pl.pallas_call(
        functools.partial(kernel, slots),
        out_shape=(
            jax.ShapeDtypeStruct((VB, 2 * TL), F32),
            jax.ShapeDtypeStruct((2, VB, VB), F32),
        ),
        in_specs=[vmem, vmem, pl.BlockSpec(memory_space=pl.ANY), smem, smem, vmem, vmem, smem],
        out_specs=(vmem, vmem),
        scratch_shapes=[
            pltpu.VMEM((slots, TL, TL), BF16),
            pltpu.VMEM((32, VB, TL), BF16),
            pltpu.VMEM((64, VB, TL), BF16),
            pltpu.VMEM((32 * VB, slots * VB), BF16),
            pltpu.VMEM((64 * VB, slots * VB), BF16),
            pltpu.VMEM((slots * VB, 2 * TL), BF16),
            pltpu.VMEM((32, VB, TL), F32),
            pltpu.VMEM((64, VB, TL), F32),
            pltpu.VMEM((32, VB, TL), F32),
            pltpu.VMEM((24, VB, TL), F32),
            pltpu.VMEM((6, VB, TL), F32),
            pltpu.VMEM((24, VB, TL), F32),
            pltpu.VMEM((6, VB, TL), F32),
            pltpu.VMEM((3, 4, TL), F32),
            pltpu.VMEM((15, 4, TL), F32),
            pltpu.VMEM((15, 4, TL), F32),
            pltpu.VMEM((4, TL), F32),
            dma,
            dma((7,)),
            dma((7,)),
            dma((7,)),
            dma((7,)),
            dma((7,)),
            dma((7,)),
            dma((7,)),
            dma((7,)),
            dma((31,)),
            dma((31,)),
        ],
        compiler_params=pltpu.CompilerParams(
            collective_id=0, has_side_effects=True, vmem_limit_bytes=32 * 2**20
        ),
    )(
        x_block,
        p_block,
        tile_values,
        tile_brow,
        tile_bcol,
        tile_brow.reshape(1, slots),
        tile_bcol.reshape(1, slots),
        tile_count,
    )


def solution(mesh):
    return jax.shard_map(
        on_device,
        mesh=mesh,
        in_specs=(
            P(None, ("row", "col")),
            P(None, ("row", "col")),
            P(("row", "col"), None, None),
            P(("row", "col")),
            P(("row", "col")),
            P(("row", "col")),
        ),
        out_specs=(P(None, ("row", "col")), P()),
        check_vma=False,
    )
```

```python
import functools

import jax
import jax.numpy as jnp
from jax import lax
from jax.experimental import pallas as pl
from jax.experimental.pallas import tpu as pltpu
from jax.sharding import PartitionSpec as P

MESH = pl.DeviceIdType.MESH
F32 = jnp.float32
BF16 = jnp.bfloat16
VB = 16
TL = 128
NT = (((1,), (1,)), ((), ()))
NN = (((1,), (0,)), ((), ()))


def iota(shape, dim):
    return lax.broadcasted_iota(jnp.int32, shape, dim)


def wide_mask():
    return iota((VB, TL), 1) // VB == iota((VB, TL), 0) % 8


def eight(block):
    return jnp.concatenate([block] * 8, axis=0)


def fold_small(ref, slot, wide):
    wide = jnp.where(wide_mask(), wide, 0.0)
    ref[slot, 0:1] = jnp.sum(wide[0:8], axis=0, keepdims=True)
    ref[slot, 1:2] = jnp.sum(wide[8:16], axis=0, keepdims=True)


def unfold_small(rows):
    upper = iota((VB, TL), 0) < 8
    wide = jnp.where(upper, jnp.broadcast_to(rows[0:1], (VB, TL)), jnp.broadcast_to(rows[1:2], (VB, TL)))
    wide = jnp.where(wide_mask(), wide, 0.0)
    turned = jnp.sum(wide.T.reshape(8, VB, VB), axis=0)
    for shift in (64, 32, 16):
        wide = wide + pltpu.roll(wide, shift, 1)
    return wide[:, 0:VB], turned


def kernel(
    slots,
    x_hbm,
    p_hbm,
    tiles_hbm,
    brow_hbm,
    bcol_hbm,
    count_s,
    images_ref,
    small_ref,
    x_ref,
    p_ref,
    brow_s,
    bcol_s,
    brow_v,
    bcol_v,
    tiles,
    near,
    far,
    kron_row,
    kron_col,
    pieces,
    down_rows,
    across_rows,
    core_in,
    x_in,
    zh_in,
    y_in,
    zl_in,
    gram,
    z_small,
    xy_small,
    corr,
    corr_in,
    load_sem,
    s_near,
    r_near,
    s_near_y,
    r_near_y,
    s_far,
    r_far,
    s_far_x,
    r_far_x,
    s_row,
    r_row,
    s_col,
    r_col,
    s_small,
    r_small,
    s_corr,
    r_corr,
):
    row, col = lax.axis_index("row"), lax.axis_index("col")
    x, zh, core = row // 8, (row // 2) % 4, row % 2
    y, zl = col // 4, col % 4

    def peer(dx=0, dy=0, dzh=0, dzl=0, dc=0):
        return (
            ((x + dx) % 4) * 8 + ((zh + dzh) % 4) * 2 + (core + dc) % 2,
            ((y + dy) % 4) * 4 + (zl + dzl) % 4,
        )

    def copy(src, dst, send, recv, to):
        return pltpu.make_async_remote_copy(
            src_ref=src, dst_ref=dst, send_sem=send, recv_sem=recv, device_id=to, device_id_type=MESH
        )

    def start(src, dst, send, recv, to):
        desc = copy(src, dst, send, recv, to)
        desc.start()
        return desc

    barrier = pltpu.get_barrier_semaphore()
    friends = (
        [peer(dzl=i) for i in (1, 2, 3)]
        + [peer(dy=i) for i in (1, 2, 3)]
        + [peer(dx=i) for i in (1, 2, 3)]
        + [peer(dzh=1), peer(dzh=3), peer(dc=1)]
    )
    for to in friends:
        pl.semaphore_signal(barrier, inc=1, device_id=to, device_id_type=MESH)

    fetches = [
        pltpu.make_async_copy(src, dst, load_sem.at[n])
        for n, (src, dst) in enumerate(
            [
                (x_hbm, x_ref),
                (p_hbm, p_ref),
                (bcol_hbm, bcol_v),
                (brow_hbm, brow_v),
                (bcol_hbm.at[0], bcol_s),
                (brow_hbm.at[0], brow_s),
                (tiles_hbm, tiles),
            ]
        )
    ]
    for fetch in fetches:
        fetch.start()
    fetches[0].wait()
    fetches[1].wait()

    for b in range(2):
        own = jnp.concatenate(
            [x_ref[:, b * TL : (b + 1) * TL].astype(F32), p_ref[:, b * TL : (b + 1) * TL].astype(F32)],
            axis=0,
        ).astype(BF16)
        near[b] = own
        far[b] = own

    pl.semaphore_wait(barrier, len(friends))
    far_x = []

    def far_spread(slot):
        for i in (2, 1, 3):
            far_x.append(
                start(
                    far.at[pl.ds(slot * 2, 2)],
                    far.at[pl.ds((4 - i) * 8 + slot * 2, 2)],
                    s_far_x.at[slot * 3 + i - 1],
                    r_far_x.at[slot * 3 + i - 1],
                    peer(dx=i),
                )
            )

    far_up = start(far.at[pl.ds(0, 2)], far.at[pl.ds(6, 2)], s_far.at[0], r_far.at[0], peer(dzh=1))
    far_dn = start(far.at[pl.ds(0, 2)], far.at[pl.ds(2, 2)], s_far.at[1], r_far.at[1], peer(dzh=3))
    near_zl = []
    for i in (3, 2, 1):
        near_zl.append(
            start(near.at[pl.ds(0, 2)], near.at[pl.ds((4 - i) * 2, 2)], s_near.at[i], r_near.at[i], peer(dzl=i))
        )
    near_y = []

    def near_spread(slot):
        for i in (2, 1, 3):
            near_y.append(
                start(
                    near.at[pl.ds(slot * 2, 2)],
                    near.at[pl.ds((4 - i) * 8 + slot * 2, 2)],
                    s_near_y.at[slot * 3 + i - 1],
                    r_near_y.at[slot * 3 + i - 1],
                    peer(dy=i),
                )
            )

    near_spread(0)
    far_spread(0)

    def place(rel):
        lane = iota((8, slots), 1)
        rel = jnp.where(lane < count_s[0], jnp.broadcast_to(rel, (8, slots)), 255)
        spread = (iota((slots, slots * VB), 1) // VB == iota((slots, slots * VB), 0)).astype(BF16)
        wide = lax.dot_general(rel.astype(F32).astype(BF16), spread, NN, preferred_element_type=F32)
        wide = jnp.concatenate([wide, wide], axis=0)
        diag = iota((VB, slots * VB), 1) % VB == iota((VB, slots * VB), 0)
        return jnp.where(diag, wide, 255.0)

    def near_index(brow):
        c = (brow // 2) % 16
        return (((c // 4 - y) & 3) * 4 + ((c % 4 - zl) & 3)) * 2 + brow % 2

    def far_index(bcol):
        m = bcol // 32
        return (
            ((((m % 2) ^ core) * 4 + ((m // 8 - x) & 3)) * 4 + (((m // 2) % 4 - zh) & 3)) * 2 + bcol % 2
        )

    def build(ref, rel, blocks):
        placed = place(rel)

        @pl.loop(0, blocks // 8)
        def _(step):
            for j in range(8):
                b = step * 8 + j
                ref[pl.ds(pl.multiple_of(b * VB, VB), VB), :] = jnp.where(
                    placed == b.astype(F32), 1.0, 0.0
                ).astype(BF16)

    for fetch in fetches[2:6]:
        fetch.wait()
    build(kron_col, far_index(bcol_v[...]), 64)
    for d, slot in zip(near_zl[::-1], (3, 2, 1)):
        d.wait_recv()
        near_spread(slot)
    far_up.wait_recv()
    far_two = start(far.at[pl.ds(6, 2)], far.at[pl.ds(4, 2)], s_far.at[2], r_far.at[2], peer(dzh=1))
    far_spread(3)
    far_dn.wait_recv()
    far_spread(1)
    build(kron_row, near_index(brow_v[...]), 32)
    fetches[6].wait()
    for d in near_y:
        d.wait_recv()

    def multiply(vec_ref, index_of, index_s, dims):
        for k in range(slots):
            part = lax.dot_general(vec_ref[index_of(index_s[k])], tiles[k], dims, preferred_element_type=F32)
            high = part.astype(BF16)
            rows = slice(k * VB, (k + 1) * VB)
            pieces[rows, 0:TL] = high
            pieces[rows, TL : 2 * TL] = (part - high.astype(F32)).astype(BF16)

    def scatter(kron, first, blocks, out_ref):
        both = lax.dot_general(
            kron[first * VB : (first + blocks) * VB, :], pieces[...], NN, preferred_element_type=F32
        )
        out_ref[first : first + blocks] = (both[:, 0:TL] + both[:, TL : 2 * TL]).reshape(blocks, VB, TL)

    multiply(near, near_index, brow_s, NN)
    scatter(kron_col, 32, 32, across_rows)
    core_rs = start(across_rows.at[pl.ds(32, 32)], core_in, s_row.at[0], r_row.at[0], peer(dc=1))
    far_two.wait_recv()
    far_spread(2)
    scatter(kron_col, 0, 32, across_rows)
    core_rs.wait_recv()
    x_rs = []
    for i in (2, 1, 3, 0):
        across_rows[i * 8 : i * 8 + 8] += core_in[i * 8 : i * 8 + 8]
        if i:
            x_rs.append(
                start(
                    across_rows.at[pl.ds(i * 8, 8)],
                    x_in.at[pl.ds((i - 1) * 8, 8)],
                    s_row.at[i],
                    r_row.at[i],
                    peer(dx=i),
                )
            )

    def share(blocks):
        high = [across_rows[b].astype(BF16) for b in blocks]
        low = [(across_rows[b] - h.astype(F32)).astype(BF16) for b, h in zip(blocks, high)]
        both = jnp.concatenate([jnp.concatenate(part, axis=1) for part in (high, low)], axis=0)
        vecs = jnp.concatenate([eight(far[b]) for b in blocks], axis=1)
        both = lax.dot_general(both, vecs, NT, preferred_element_type=F32)
        return both[0:VB] + both[VB : 2 * VB]

    for d in far_x[:9]:
        d.wait_recv()
    half = share([b for b in range(32) if b % 8 // 2 != 2])
    for d in far_x[9:]:
        d.wait_recv()
    half = half + share([b for b in range(32) if b % 8 // 2 == 2])
    far_core = start(far.at[pl.ds(0, 32)], far.at[pl.ds(32, 32)], s_far.at[6], r_far.at[6], peer(dc=1))
    fold_small(gram, 0, half)
    small_z = []
    for n in range(1, 16):
        zz = zh * 4 + zl + n
        to = (x * 8 + ((zz // 4) % 4) * 2 + core, y * 4 + zz % 4)
        small_z.append(start(gram.at[0], z_small.at[n - 1], s_small.at[n - 1], r_small.at[n - 1], to))

    far_core.wait_recv()
    multiply(far, far_index, bcol_s, NT)
    scatter(kron_row, 8, 24, down_rows)
    y_rs = []
    for i in (2, 1, 3):
        y_rs.append(
            start(
                down_rows.at[pl.ds(i * 8, 8)], y_in.at[pl.ds((i - 1) * 8, 8)], s_col.at[i], r_col.at[i], peer(dy=i)
            )
        )
    scatter(kron_row, 0, 8, down_rows)
    wide = jnp.concatenate([near[b] for b in range(32)], axis=1)
    tall = jnp.concatenate([eight(near[b]) for b in range(32)], axis=1)
    fold_small(corr, 0, lax.dot_general(wide, tall, NT, preferred_element_type=F32))
    corr_core = start(corr.at[0], corr_in.at[0], s_corr.at[0], r_corr.at[0], peer(dc=1))
    for d in x_rs:
        d.wait_recv()
    zh_rs = []
    for i in (2, 1, 3, 0):
        mine = pl.ds(i * 2, 2)
        across_rows[mine] += x_in[i * 2 : i * 2 + 2] + x_in[8 + i * 2 : 10 + i * 2] + x_in[16 + i * 2 : 18 + i * 2]
        if i:
            zh_rs.append(
                start(across_rows.at[mine], zh_in.at[pl.ds((i - 1) * 2, 2)], s_row.at[3 + i], r_row.at[3 + i], peer(dzh=i))
            )
    corr_core.wait_recv()
    corr[1] = corr[0] + corr_in[0]
    corr_x = [start(corr.at[1], corr_in.at[i], s_corr.at[i], r_corr.at[i], peer(dx=i)) for i in (1, 2, 3)]

    for d in y_rs:
        d.wait_recv()
    zl_rs = []
    for i in (3, 2, 1, 0):
        mine = pl.ds(i * 2, 2)
        down_rows[mine] += y_in[i * 2 : i * 2 + 2] + y_in[8 + i * 2 : 10 + i * 2] + y_in[16 + i * 2 : 18 + i * 2]
        if i:
            zl_rs.append(
                start(down_rows.at[mine], zl_in.at[pl.ds((i - 1) * 2, 2)], s_col.at[3 + i], r_col.at[3 + i], peer(dzl=i))
            )

    for d in corr_x:
        d.wait_recv()
    corr[2] = corr[1] + (corr_in[1] + corr_in[2] + corr_in[3])
    corr_zh = [start(corr.at[2], corr_in.at[3 + i], s_corr.at[3 + i], r_corr.at[3 + i], peer(dzh=i)) for i in (1, 2, 3)]

    for d in small_z:
        d.wait_recv()
    gram[1] = gram[0] + jnp.sum(z_small[...], axis=0)
    small_xy = []
    for n in (20, 21, 4, 5, 16, 17, 12, 13, 18, 19, 22, 23, 28, 29, 2, 3, 6, 7, 8, 9, 24, 25, 10, 11, 14, 15, 26, 27, 30, 31, 1):
        to = peer(dx=n // 8, dy=(n // 2) % 4, dc=n % 2)
        small_xy.append(start(gram.at[1], xy_small.at[n - 1], s_small.at[14 + n], r_small.at[14 + n], to))

    scale = 1.0 / (1024 * TL)
    for d in zl_rs + zh_rs + corr_zh:
        d.wait_recv()
    for b in range(2):
        images_ref[:, b * TL : (b + 1) * TL] = (
            (down_rows[b] + across_rows[b])
            + ((zl_in[b] + zl_in[2 + b] + zl_in[4 + b]) + (zh_in[b] + zh_in[2 + b] + zh_in[4 + b]))
        )
    small_ref[1] = unfold_small((corr[2] + (corr_in[4] + corr_in[5] + corr_in[6])) * scale)[0]

    for d in (
        [far_up, far_dn, far_two, far_core, core_rs, corr_core]
        + near_zl + near_y + far_x + x_rs + zh_rs + y_rs + zl_rs + corr_x + corr_zh + small_z
    ):
        d.wait_send()
    for d in small_xy:
        d.wait_recv()
    straight, turned = unfold_small((gram[1] + jnp.sum(xy_small[...], axis=0)) * scale)
    small_ref[0] = straight + turned
    for d in small_xy:
        d.wait_send()


def on_device(x_block, p_block, tile_values, tile_brow, tile_bcol, tile_count):
    slots = tile_values.shape[0]
    vmem = pl.BlockSpec(memory_space=pltpu.VMEM)
    dma = pltpu.SemaphoreType.DMA
    return pl.pallas_call(
        functools.partial(kernel, slots),
        out_shape=(
            jax.ShapeDtypeStruct((VB, 2 * TL), F32),
            jax.ShapeDtypeStruct((2, VB, VB), F32),
        ),
        in_specs=[pl.BlockSpec(memory_space=pltpu.HBM)] * 5 + [pl.BlockSpec(memory_space=pltpu.SMEM)],
        out_specs=(vmem, vmem),
        scratch_shapes=[
            pltpu.VMEM((8, 2 * TL), BF16),
            pltpu.VMEM((8, 2 * TL), BF16),
            pltpu.SMEM((slots,), jnp.int32),
            pltpu.SMEM((slots,), jnp.int32),
            pltpu.VMEM((1, slots), jnp.int32),
            pltpu.VMEM((1, slots), jnp.int32),
            pltpu.VMEM((slots, TL, TL), BF16),
            pltpu.VMEM((32, VB, TL), BF16),
            pltpu.VMEM((64, VB, TL), BF16),
            pltpu.VMEM((32 * VB, slots * VB), BF16),
            pltpu.VMEM((64 * VB, slots * VB), BF16),
            pltpu.VMEM((slots * VB, 2 * TL), BF16),
            pltpu.VMEM((32, VB, TL), F32),
            pltpu.VMEM((64, VB, TL), F32),
            pltpu.VMEM((32, VB, TL), F32),
            pltpu.VMEM((24, VB, TL), F32),
            pltpu.VMEM((6, VB, TL), F32),
            pltpu.VMEM((24, VB, TL), F32),
            pltpu.VMEM((6, VB, TL), F32),
            pltpu.VMEM((2, 2, TL), F32),
            pltpu.VMEM((15, 2, TL), F32),
            pltpu.VMEM((31, 2, TL), F32),
            pltpu.VMEM((3, 2, TL), F32),
            pltpu.VMEM((7, 2, TL), F32),
            dma((7,)),
            dma((4,)),
            dma((4,)),
            dma((12,)),
            dma((12,)),
            dma((7,)),
            dma((7,)),
            dma((12,)),
            dma((12,)),
            dma((7,)),
            dma((7,)),
            dma((7,)),
            dma((7,)),
            dma((46,)),
            dma((46,)),
            dma((7,)),
            dma((7,)),
        ],
        compiler_params=pltpu.CompilerParams(
            collective_id=0, has_side_effects=True, vmem_limit_bytes=32 * 2**20
        ),
    )(
        *(
            pltpu.with_memory_space_constraint(arg, pltpu.HBM)
            for arg in (
                x_block,
                p_block,
                tile_values,
                tile_brow.reshape(1, slots),
                tile_bcol.reshape(1, slots),
            )
        ),
        tile_count,
    )


def solution(mesh):
    return jax.shard_map(
        on_device,
        mesh=mesh,
        in_specs=(
            P(None, ("row", "col")),
            P(None, ("row", "col")),
            P(("row", "col"), None, None),
            P(("row", "col")),
            P(("row", "col")),
            P(("row", "col")),
        ),
        out_specs=(P(None, ("row", "col")), P()),
        check_vma=False,
    )
```

```python
import functools

import jax
import jax.numpy as jnp
from jax import lax
from jax.experimental import pallas as pl
from jax.experimental.pallas import tpu as pltpu
from jax.sharding import PartitionSpec as P

MESH = pl.DeviceIdType.MESH
F32 = jnp.float32
BF16 = jnp.bfloat16
VB = 16
TL = 128
NT = (((1,), (1,)), ((), ()))
NN = (((1,), (0,)), ((), ()))


def iota(shape, dim):
    return lax.broadcasted_iota(jnp.int32, shape, dim)


def wide_mask():
    return iota((VB, TL), 1) // VB == iota((VB, TL), 0) % 8


def eight(block):
    return jnp.concatenate([block] * 8, axis=0)


def fold_small(ref, slot, wide):
    wide = jnp.where(wide_mask(), wide, 0.0)
    ref[slot, 0:1] = jnp.sum(wide[0:8], axis=0, keepdims=True)
    ref[slot, 1:2] = jnp.sum(wide[8:16], axis=0, keepdims=True)


def unfold_small(rows):
    upper = iota((VB, TL), 0) < 8
    wide = jnp.where(upper, jnp.broadcast_to(rows[0:1], (VB, TL)), jnp.broadcast_to(rows[1:2], (VB, TL)))
    wide = jnp.where(wide_mask(), wide, 0.0)
    turned = jnp.sum(wide.T.reshape(8, VB, VB), axis=0)
    for shift in (64, 32, 16):
        wide = wide + pltpu.roll(wide, shift, 1)
    return wide[:, 0:VB], turned


def kernel(
    slots,
    x_hbm,
    p_hbm,
    tiles_hbm,
    brow_hbm,
    bcol_hbm,
    count_s,
    images_ref,
    small_ref,
    x_ref,
    p_ref,
    brow_s,
    bcol_s,
    brow_v,
    bcol_v,
    tiles,
    near,
    far,
    kron_row,
    kron_col,
    pieces,
    down_rows,
    across_rows,
    core_in,
    x_in,
    zh_in,
    y_in,
    zl_in,
    gram,
    z_small,
    xy_small,
    corr,
    corr_in,
    load_sem,
    s_near,
    r_near,
    s_near_y,
    r_near_y,
    s_far,
    r_far,
    s_far_x,
    r_far_x,
    s_row,
    r_row,
    s_col,
    r_col,
    s_small,
    r_small,
    s_corr,
    r_corr,
):
    row, col = lax.axis_index("row"), lax.axis_index("col")
    x, zh, core = row // 8, (row // 2) % 4, row % 2
    y, zl = col // 4, col % 4

    def peer(dx=0, dy=0, dzh=0, dzl=0, dc=0):
        return (
            ((x + dx) % 4) * 8 + ((zh + dzh) % 4) * 2 + (core + dc) % 2,
            ((y + dy) % 4) * 4 + (zl + dzl) % 4,
        )

    def copy(src, dst, send, recv, to):
        return pltpu.make_async_remote_copy(
            src_ref=src, dst_ref=dst, send_sem=send, recv_sem=recv, device_id=to, device_id_type=MESH
        )

    def start(src, dst, send, recv, to):
        desc = copy(src, dst, send, recv, to)
        desc.start()
        return desc

    barrier = pltpu.get_barrier_semaphore()
    friends = (
        [peer(dzl=i) for i in (1, 2, 3)]
        + [peer(dy=i) for i in (1, 2, 3)]
        + [peer(dx=i, dc=dc) for i in (1, 2, 3) for dc in (0, 1)]
        + [peer(dzh=1), peer(dzh=3), peer(dc=1)]
    )
    for to in friends:
        pl.semaphore_signal(barrier, inc=1, device_id=to, device_id_type=MESH)

    fetches = [
        pltpu.make_async_copy(src, dst, load_sem.at[n])
        for n, (src, dst) in enumerate(
            [
                (x_hbm, x_ref),
                (p_hbm, p_ref),
                (bcol_hbm, bcol_v),
                (brow_hbm, brow_v),
                (bcol_hbm.at[0], bcol_s),
                (brow_hbm.at[0], brow_s),
                (tiles_hbm, tiles),
            ]
        )
    ]
    for fetch in fetches:
        fetch.start()
    fetches[0].wait()
    fetches[1].wait()

    for b in range(2):
        own = jnp.concatenate(
            [x_ref[:, b * TL : (b + 1) * TL].astype(F32), p_ref[:, b * TL : (b + 1) * TL].astype(F32)],
            axis=0,
        ).astype(BF16)
        near[b] = own
        far[b] = own

    pl.semaphore_wait(barrier, len(friends))
    far_x = []

    def far_spread(slot):
        block = far.at[pl.ds(slot * 2, 2)]
        for n in (2, 6, 1, 3, 5, 7, 4):
            i, dc = n % 4, n // 4
            place = pl.ds(dc * 32 + (4 - i) % 4 * 8 + slot * 2, 2)
            far_x.append(
                start(block, far.at[place], s_far_x.at[slot * 7 + n - 1], r_far_x.at[slot * 7 + n - 1], peer(dx=i, dc=dc))
            )

    far_up = start(far.at[pl.ds(0, 2)], far.at[pl.ds(6, 2)], s_far.at[0], r_far.at[0], peer(dzh=1))
    far_dn = start(far.at[pl.ds(0, 2)], far.at[pl.ds(2, 2)], s_far.at[1], r_far.at[1], peer(dzh=3))
    near_zl = []
    for i in (3, 2, 1):
        near_zl.append(
            start(near.at[pl.ds(0, 2)], near.at[pl.ds((4 - i) * 2, 2)], s_near.at[i], r_near.at[i], peer(dzl=i))
        )
    near_y = []

    def near_spread(slot):
        for i in (2, 1, 3):
            near_y.append(
                start(
                    near.at[pl.ds(slot * 2, 2)],
                    near.at[pl.ds((4 - i) * 8 + slot * 2, 2)],
                    s_near_y.at[slot * 3 + i - 1],
                    r_near_y.at[slot * 3 + i - 1],
                    peer(dy=i),
                )
            )

    near_spread(0)
    far_spread(0)

    def place(rel):
        lane = iota((8, slots), 1)
        rel = jnp.where(lane < count_s[0], jnp.broadcast_to(rel, (8, slots)), 255)
        spread = (iota((slots, slots * VB), 1) // VB == iota((slots, slots * VB), 0)).astype(BF16)
        wide = lax.dot_general(rel.astype(F32).astype(BF16), spread, NN, preferred_element_type=F32)
        wide = jnp.concatenate([wide, wide], axis=0)
        diag = iota((VB, slots * VB), 1) % VB == iota((VB, slots * VB), 0)
        return jnp.where(diag, wide, 255.0)

    def near_index(brow):
        c = (brow // 2) % 16
        return (((c // 4 - y) & 3) * 4 + ((c % 4 - zl) & 3)) * 2 + brow % 2

    def far_index(bcol):
        m = bcol // 32
        return (
            ((((m % 2) ^ core) * 4 + ((m // 8 - x) & 3)) * 4 + (((m // 2) % 4 - zh) & 3)) * 2 + bcol % 2
        )

    def build(ref, rel, blocks):
        placed = place(rel)

        @pl.loop(0, blocks // 8)
        def _(step):
            for j in range(8):
                b = step * 8 + j
                ref[pl.ds(pl.multiple_of(b * VB, VB), VB), :] = jnp.where(
                    placed == b.astype(F32), 1.0, 0.0
                ).astype(BF16)

    for fetch in fetches[2:6]:
        fetch.wait()
    build(kron_col, far_index(bcol_v[...]), 64)
    for d, slot in zip(near_zl[::-1], (3, 2, 1)):
        d.wait_recv()
        near_spread(slot)
    far_up.wait_recv()
    far_two = start(far.at[pl.ds(6, 2)], far.at[pl.ds(4, 2)], s_far.at[2], r_far.at[2], peer(dzh=1))
    far_spread(3)
    far_dn.wait_recv()
    far_spread(1)
    build(kron_row, near_index(brow_v[...]), 32)
    fetches[6].wait()
    for d in near_y:
        d.wait_recv()

    def multiply(vec_ref, index_of, index_s, dims):
        for k in range(slots):
            part = lax.dot_general(vec_ref[index_of(index_s[k])], tiles[k], dims, preferred_element_type=F32)
            high = part.astype(BF16)
            rows = slice(k * VB, (k + 1) * VB)
            pieces[rows, 0:TL] = high
            pieces[rows, TL : 2 * TL] = (part - high.astype(F32)).astype(BF16)

    def scatter(kron, first, blocks, out_ref):
        both = lax.dot_general(
            kron[first * VB : (first + blocks) * VB, :], pieces[...], NN, preferred_element_type=F32
        )
        out_ref[first : first + blocks] = (both[:, 0:TL] + both[:, TL : 2 * TL]).reshape(blocks, VB, TL)

    multiply(near, near_index, brow_s, NN)
    far_two.wait_recv()
    far_spread(2)
    scatter(kron_col, 32, 32, across_rows)
    core_rs = start(across_rows.at[pl.ds(32, 32)], core_in, s_row.at[0], r_row.at[0], peer(dc=1))
    scatter(kron_col, 0, 32, across_rows)
    core_rs.wait_recv()
    x_rs = []
    for i in (2, 1, 3, 0):
        across_rows[i * 8 : i * 8 + 8] += core_in[i * 8 : i * 8 + 8]
        if i:
            x_rs.append(
                start(
                    across_rows.at[pl.ds(i * 8, 8)],
                    x_in.at[pl.ds((i - 1) * 8, 8)],
                    s_row.at[i],
                    r_row.at[i],
                    peer(dx=i),
                )
            )

    def share(blocks):
        high = [across_rows[b].astype(BF16) for b in blocks]
        low = [(across_rows[b] - h.astype(F32)).astype(BF16) for b, h in zip(blocks, high)]
        both = jnp.concatenate([jnp.concatenate(part, axis=1) for part in (high, low)], axis=0)
        vecs = jnp.concatenate([eight(far[b]) for b in blocks], axis=1)
        both = lax.dot_general(both, vecs, NT, preferred_element_type=F32)
        return both[0:VB] + both[VB : 2 * VB]

    wide = jnp.concatenate([near[b] for b in range(32)], axis=1)
    tall = jnp.concatenate([eight(near[b]) for b in range(32)], axis=1)
    fold_small(corr, 0, lax.dot_general(wide, tall, NT, preferred_element_type=F32))
    corr_core = start(corr.at[0], corr_in.at[0], s_corr.at[0], r_corr.at[0], peer(dc=1))
    for d in far_x[:21]:
        d.wait_recv()
    half = share([b for b in range(32) if b % 8 // 2 != 2])
    for d in far_x[21:]:
        d.wait_recv()
    half = half + share([b for b in range(32) if b % 8 // 2 == 2])
    fold_small(gram, 0, half)
    small_z = []
    for n in range(1, 16):
        zz = zh * 4 + zl + n
        to = (x * 8 + ((zz // 4) % 4) * 2 + core, y * 4 + zz % 4)
        small_z.append(start(gram.at[0], z_small.at[n - 1], s_small.at[n - 1], r_small.at[n - 1], to))

    corr_core.wait_recv()
    corr[1] = corr[0] + corr_in[0]
    corr_x = [start(corr.at[1], corr_in.at[i], s_corr.at[i], r_corr.at[i], peer(dx=i)) for i in (1, 2, 3)]
    multiply(far, far_index, bcol_s, NT)
    scatter(kron_row, 8, 24, down_rows)
    y_rs = []
    for i in (2, 1, 3):
        y_rs.append(
            start(
                down_rows.at[pl.ds(i * 8, 8)], y_in.at[pl.ds((i - 1) * 8, 8)], s_col.at[i], r_col.at[i], peer(dy=i)
            )
        )
    scatter(kron_row, 0, 8, down_rows)
    for d in x_rs:
        d.wait_recv()
    zh_rs = []
    for i in (2, 1, 3, 0):
        mine = pl.ds(i * 2, 2)
        across_rows[mine] += x_in[i * 2 : i * 2 + 2] + x_in[8 + i * 2 : 10 + i * 2] + x_in[16 + i * 2 : 18 + i * 2]
        if i:
            zh_rs.append(
                start(across_rows.at[mine], zh_in.at[pl.ds((i - 1) * 2, 2)], s_row.at[3 + i], r_row.at[3 + i], peer(dzh=i))
            )
    for d in corr_x:
        d.wait_recv()
    corr[2] = corr[1] + (corr_in[1] + corr_in[2] + corr_in[3])
    corr_zh = [start(corr.at[2], corr_in.at[3 + i], s_corr.at[3 + i], r_corr.at[3 + i], peer(dzh=i)) for i in (1, 2, 3)]

    for d in y_rs:
        d.wait_recv()
    zl_rs = []
    for i in (3, 2, 1, 0):
        mine = pl.ds(i * 2, 2)
        down_rows[mine] += y_in[i * 2 : i * 2 + 2] + y_in[8 + i * 2 : 10 + i * 2] + y_in[16 + i * 2 : 18 + i * 2]
        if i:
            zl_rs.append(
                start(down_rows.at[mine], zl_in.at[pl.ds((i - 1) * 2, 2)], s_col.at[3 + i], r_col.at[3 + i], peer(dzl=i))
            )

    for d in small_z:
        d.wait_recv()
    gram[1] = gram[0] + jnp.sum(z_small[...], axis=0)
    small_xy = []
    for n in (20, 21, 4, 5, 16, 17, 12, 13, 18, 19, 22, 23, 28, 29, 2, 3, 6, 7, 8, 9, 24, 25, 10, 11, 14, 15, 26, 27, 30, 31, 1):
        to = peer(dx=n // 8, dy=(n // 2) % 4, dc=n % 2)
        small_xy.append(start(gram.at[1], xy_small.at[n - 1], s_small.at[14 + n], r_small.at[14 + n], to))

    scale = 1.0 / (1024 * TL)
    for d in zl_rs + zh_rs + corr_zh:
        d.wait_recv()
    for b in range(2):
        images_ref[:, b * TL : (b + 1) * TL] = (
            (down_rows[b] + across_rows[b])
            + ((zl_in[b] + zl_in[2 + b] + zl_in[4 + b]) + (zh_in[b] + zh_in[2 + b] + zh_in[4 + b]))
        )
    small_ref[1] = unfold_small((corr[2] + (corr_in[4] + corr_in[5] + corr_in[6])) * scale)[0]

    for d in (
        [far_up, far_dn, far_two, core_rs, corr_core]
        + near_zl + near_y + far_x + x_rs + zh_rs + y_rs + zl_rs + corr_x + corr_zh + small_z
    ):
        d.wait_send()
    for d in small_xy:
        d.wait_recv()
    straight, turned = unfold_small((gram[1] + jnp.sum(xy_small[...], axis=0)) * scale)
    small_ref[0] = straight + turned
    for d in small_xy:
        d.wait_send()


def on_device(x_block, p_block, tile_values, tile_brow, tile_bcol, tile_count):
    slots = tile_values.shape[0]
    vmem = pl.BlockSpec(memory_space=pltpu.VMEM)
    dma = pltpu.SemaphoreType.DMA
    return pl.pallas_call(
        functools.partial(kernel, slots),
        out_shape=(
            jax.ShapeDtypeStruct((VB, 2 * TL), F32),
            jax.ShapeDtypeStruct((2, VB, VB), F32),
        ),
        in_specs=[pl.BlockSpec(memory_space=pltpu.HBM)] * 5 + [pl.BlockSpec(memory_space=pltpu.SMEM)],
        out_specs=(vmem, vmem),
        scratch_shapes=[
            pltpu.VMEM((8, 2 * TL), BF16),
            pltpu.VMEM((8, 2 * TL), BF16),
            pltpu.SMEM((slots,), jnp.int32),
            pltpu.SMEM((slots,), jnp.int32),
            pltpu.VMEM((1, slots), jnp.int32),
            pltpu.VMEM((1, slots), jnp.int32),
            pltpu.VMEM((slots, TL, TL), BF16),
            pltpu.VMEM((32, VB, TL), BF16),
            pltpu.VMEM((64, VB, TL), BF16),
            pltpu.VMEM((32 * VB, slots * VB), BF16),
            pltpu.VMEM((64 * VB, slots * VB), BF16),
            pltpu.VMEM((slots * VB, 2 * TL), BF16),
            pltpu.VMEM((32, VB, TL), F32),
            pltpu.VMEM((64, VB, TL), F32),
            pltpu.VMEM((32, VB, TL), F32),
            pltpu.VMEM((24, VB, TL), F32),
            pltpu.VMEM((6, VB, TL), F32),
            pltpu.VMEM((24, VB, TL), F32),
            pltpu.VMEM((6, VB, TL), F32),
            pltpu.VMEM((2, 2, TL), F32),
            pltpu.VMEM((15, 2, TL), F32),
            pltpu.VMEM((31, 2, TL), F32),
            pltpu.VMEM((3, 2, TL), F32),
            pltpu.VMEM((7, 2, TL), F32),
            dma((7,)),
            dma((4,)),
            dma((4,)),
            dma((12,)),
            dma((12,)),
            dma((3,)),
            dma((3,)),
            dma((28,)),
            dma((28,)),
            dma((7,)),
            dma((7,)),
            dma((7,)),
            dma((7,)),
            dma((46,)),
            dma((46,)),
            dma((7,)),
            dma((7,)),
        ],
        compiler_params=pltpu.CompilerParams(
            collective_id=0, has_side_effects=True, vmem_limit_bytes=32 * 2**20
        ),
    )(
        *(
            pltpu.with_memory_space_constraint(arg, pltpu.HBM)
            for arg in (
                x_block,
                p_block,
                tile_values,
                tile_brow.reshape(1, slots),
                tile_bcol.reshape(1, slots),
            )
        ),
        tile_count,
    )


def solution(mesh):
    return jax.shard_map(
        on_device,
        mesh=mesh,
        in_specs=(
            P(None, ("row", "col")),
            P(None, ("row", "col")),
            P(("row", "col"), None, None),
            P(("row", "col")),
            P(("row", "col")),
            P(("row", "col")),
        ),
        out_specs=(P(None, ("row", "col")), P()),
        check_vma=False,
    )
```

```python
import functools

import jax
import jax.numpy as jnp
from jax import lax
from jax.experimental import pallas as pl
from jax.experimental.pallas import tpu as pltpu
from jax.sharding import PartitionSpec as P

MESH = pl.DeviceIdType.MESH
F32 = jnp.float32
BF16 = jnp.bfloat16
VB = 16
TL = 128
NT = (((1,), (1,)), ((), ()))
NN = (((1,), (0,)), ((), ()))


def iota(shape, dim):
    return lax.broadcasted_iota(jnp.int32, shape, dim)


def wide_mask():
    return iota((VB, TL), 1) // VB == iota((VB, TL), 0) % 8


def eight(block):
    return jnp.concatenate([block] * 8, axis=0)


def fold_small(ref, slot, wide):
    wide = jnp.where(wide_mask(), wide, 0.0)
    ref[slot, 0:1] = jnp.sum(wide[0:8], axis=0, keepdims=True)
    ref[slot, 1:2] = jnp.sum(wide[8:16], axis=0, keepdims=True)


def unfold_small(rows):
    upper = iota((VB, TL), 0) < 8
    wide = jnp.where(upper, jnp.broadcast_to(rows[0:1], (VB, TL)), jnp.broadcast_to(rows[1:2], (VB, TL)))
    wide = jnp.where(wide_mask(), wide, 0.0)
    turned = jnp.sum(wide.T.reshape(8, VB, VB), axis=0)
    for shift in (64, 32, 16):
        wide = wide + pltpu.roll(wide, shift, 1)
    return wide[:, 0:VB], turned


def kernel(
    slots,
    x_hbm,
    p_hbm,
    tiles_hbm,
    brow_hbm,
    bcol_hbm,
    count_s,
    images_ref,
    small_ref,
    x_ref,
    p_ref,
    brow_s,
    bcol_s,
    brow_v,
    bcol_v,
    tiles,
    near,
    far,
    kron_row,
    kron_col,
    pieces,
    down_rows,
    across_rows,
    core_in,
    x_in,
    zh_in,
    y_in,
    zl_in,
    gram,
    z_small,
    xy_small,
    corr,
    corr_in,
    load_sem,
    s_near,
    r_near,
    s_far,
    r_far,
    s_far_x,
    r_far_x,
    s_row,
    r_row,
    s_col,
    r_col,
    s_small,
    r_small,
    s_corr,
    r_corr,
):
    row, col = lax.axis_index("row"), lax.axis_index("col")
    x, zh, core = row // 8, (row // 2) % 4, row % 2
    y, zl = col // 4, col % 4

    def peer(dx=0, dy=0, dzh=0, dzl=0, dc=0):
        return (
            ((x + dx) % 4) * 8 + ((zh + dzh) % 4) * 2 + (core + dc) % 2,
            ((y + dy) % 4) * 4 + (zl + dzl) % 4,
        )

    def copy(src, dst, send, recv, to):
        return pltpu.make_async_remote_copy(
            src_ref=src, dst_ref=dst, send_sem=send, recv_sem=recv, device_id=to, device_id_type=MESH
        )

    def start(src, dst, send, recv, to):
        desc = copy(src, dst, send, recv, to)
        desc.start()
        return desc

    def received(region, sem):
        copy(region, region, sem, sem, peer(dc=1)).wait_recv()

    def left(region, sem):
        copy(region, region, sem, sem, peer(dc=1)).wait_send()

    barrier = pltpu.get_barrier_semaphore()
    friends = (
        [peer(dzl=i) for i in (1, 2, 3)]
        + [peer(dy=i) for i in (1, 2, 3)]
        + [peer(dx=i, dc=dc) for i in (1, 2, 3) for dc in (0, 1)]
        + [peer(dzh=1), peer(dzh=3), peer(dc=1)]
    )
    for to in friends:
        pl.semaphore_signal(barrier, inc=1, device_id=to, device_id_type=MESH)

    fetches = [
        pltpu.make_async_copy(src, dst, load_sem.at[n])
        for n, (src, dst) in enumerate(
            [
                (x_hbm, x_ref),
                (p_hbm, p_ref),
                (bcol_hbm, bcol_v),
                (brow_hbm, brow_v),
                (bcol_hbm.at[0], bcol_s),
                (brow_hbm.at[0], brow_s),
                (tiles_hbm, tiles),
            ]
        )
    ]
    for fetch in fetches:
        fetch.start()
    fetches[0].wait()
    fetches[1].wait()

    for b in range(2):
        own = jnp.concatenate(
            [x_ref[:, b * TL : (b + 1) * TL].astype(F32), p_ref[:, b * TL : (b + 1) * TL].astype(F32)],
            axis=0,
        ).astype(BF16)
        near[b] = own
        far[b] = own

    pl.semaphore_wait(barrier, len(friends))
    def far_spread(slot):
        block = far.at[pl.ds(slot * 2, 2)]
        for n in (2, 6, 1, 3, 5, 7, 4):
            i, dc = n % 4, n // 4
            place = pl.ds(dc * 32 + (4 - i) % 4 * 8 + slot * 2, 2)
            late = int(slot == 2)
            start(block, far.at[place], s_far_x.at[late], r_far_x.at[late], peer(dx=i, dc=dc))

    far_up = start(far.at[pl.ds(0, 2)], far.at[pl.ds(6, 2)], s_far.at[0], r_far.at[0], peer(dzh=1))
    far_dn = start(far.at[pl.ds(0, 2)], far.at[pl.ds(2, 2)], s_far.at[1], r_far.at[1], peer(dzh=3))
    near_zl = []
    for i in (3, 2, 1):
        near_zl.append(
            start(near.at[pl.ds(0, 2)], near.at[pl.ds((4 - i) * 2, 2)], s_near.at[i], r_near.at[i], peer(dzl=i))
        )

    def near_spread(slot):
        for i in (2, 1, 3):
            place = pl.ds((4 - i) * 8 + slot * 2, 2)
            start(near.at[pl.ds(slot * 2, 2)], near.at[place], s_near.at[0], r_near.at[0], peer(dy=i))

    near_spread(0)
    far_spread(0)

    def place(rel):
        lane = iota((8, slots), 1)
        rel = jnp.where(lane < count_s[0], jnp.broadcast_to(rel, (8, slots)), 255)
        spread = (iota((slots, slots * VB), 1) // VB == iota((slots, slots * VB), 0)).astype(BF16)
        wide = lax.dot_general(rel.astype(F32).astype(BF16), spread, NN, preferred_element_type=F32)
        wide = jnp.concatenate([wide, wide], axis=0)
        diag = iota((VB, slots * VB), 1) % VB == iota((VB, slots * VB), 0)
        return jnp.where(diag, wide, 255.0)

    def near_index(brow):
        c = (brow // 2) % 16
        return (((c // 4 - y) & 3) * 4 + ((c % 4 - zl) & 3)) * 2 + brow % 2

    def far_index(bcol):
        m = bcol // 32
        return (
            ((((m % 2) ^ core) * 4 + ((m // 8 - x) & 3)) * 4 + (((m // 2) % 4 - zh) & 3)) * 2 + bcol % 2
        )

    def build(ref, rel, blocks):
        placed = place(rel)

        @pl.loop(0, blocks // 8)
        def _(step):
            for j in range(8):
                b = step * 8 + j
                ref[pl.ds(pl.multiple_of(b * VB, VB), VB), :] = jnp.where(
                    placed == b.astype(F32), 1.0, 0.0
                ).astype(BF16)

    for fetch in fetches[2:6]:
        fetch.wait()
    build(kron_col, far_index(bcol_v[...]), 64)
    for d, slot in zip(near_zl[::-1], (3, 2, 1)):
        d.wait_recv()
        near_spread(slot)
    far_up.wait_recv()
    far_two = start(far.at[pl.ds(6, 2)], far.at[pl.ds(4, 2)], s_far.at[2], r_far.at[2], peer(dzh=1))
    far_spread(3)
    far_dn.wait_recv()
    far_spread(1)
    build(kron_row, near_index(brow_v[...]), 32)
    fetches[6].wait()
    received(near.at[pl.ds(8, 24)], r_near.at[0])

    def multiply(vec_ref, index_of, index_s, dims):
        for k in range(slots):
            part = lax.dot_general(vec_ref[index_of(index_s[k])], tiles[k], dims, preferred_element_type=F32)
            high = part.astype(BF16)
            rows = slice(k * VB, (k + 1) * VB)
            pieces[rows, 0:TL] = high
            pieces[rows, TL : 2 * TL] = (part - high.astype(F32)).astype(BF16)

    def scatter(kron, first, blocks, out_ref):
        both = lax.dot_general(
            kron[first * VB : (first + blocks) * VB, :], pieces[...], NN, preferred_element_type=F32
        )
        out_ref[first : first + blocks] = (both[:, 0:TL] + both[:, TL : 2 * TL]).reshape(blocks, VB, TL)

    multiply(near, near_index, brow_s, NN)
    far_two.wait_recv()
    far_spread(2)
    scatter(kron_col, 32, 32, across_rows)
    core_rs = start(across_rows.at[pl.ds(32, 32)], core_in, s_row.at[0], r_row.at[0], peer(dc=1))
    scatter(kron_col, 0, 32, across_rows)
    core_rs.wait_recv()
    for i in (2, 1, 3, 0):
        mine = pl.ds(i * 8, 8)
        across_rows[mine] += core_in[mine]
        if i:
            start(across_rows.at[mine], x_in.at[pl.ds((i - 1) * 8, 8)], s_row.at[1], r_row.at[1], peer(dx=i))

    def share(blocks):
        high = [across_rows[b].astype(BF16) for b in blocks]
        low = [(across_rows[b] - h.astype(F32)).astype(BF16) for b, h in zip(blocks, high)]
        both = jnp.concatenate([jnp.concatenate(part, axis=1) for part in (high, low)], axis=0)
        vecs = jnp.concatenate([eight(far[b]) for b in blocks], axis=1)
        both = lax.dot_general(both, vecs, NT, preferred_element_type=F32)
        return both[0:VB] + both[VB : 2 * VB]

    wide = jnp.concatenate([near[b] for b in range(32)], axis=1)
    tall = jnp.concatenate([eight(near[b]) for b in range(32)], axis=1)
    fold_small(corr, 0, lax.dot_general(wide, tall, NT, preferred_element_type=F32))
    corr_core = start(corr.at[0], corr_in.at[0], s_corr.at[0], r_corr.at[0], peer(dc=1))
    received(far.at[pl.ds(0, 42)], r_far_x.at[0])
    half = share([b for b in range(32) if b % 8 // 2 != 2])
    received(far.at[pl.ds(0, 14)], r_far_x.at[1])
    half = half + share([b for b in range(32) if b % 8 // 2 == 2])
    fold_small(gram, 0, half)
    for n in (8, 7, 9, 6, 10, 5, 11, 4, 12, 3, 13, 2, 14, 1, 15):
        zz = zh * 4 + zl + n
        to = (x * 8 + ((zz // 4) % 4) * 2 + core, y * 4 + zz % 4)
        start(gram.at[0], z_small.at[n - 1], s_small.at[0], r_small.at[0], to)

    corr_core.wait_recv()
    corr[1] = corr[0] + corr_in[0]
    for i in (1, 2, 3):
        start(corr.at[1], corr_in.at[i], s_corr.at[1], r_corr.at[1], peer(dx=i))
    multiply(far, far_index, bcol_s, NT)
    scatter(kron_row, 8, 24, down_rows)
    for i in (2, 1, 3):
        start(down_rows.at[pl.ds(i * 8, 8)], y_in.at[pl.ds((i - 1) * 8, 8)], s_col.at[0], r_col.at[0], peer(dy=i))
    scatter(kron_row, 0, 8, down_rows)
    received(x_in, r_row.at[1])
    for i in (2, 1, 3, 0):
        mine = pl.ds(i * 2, 2)
        across_rows[mine] += x_in[i * 2 : i * 2 + 2] + x_in[8 + i * 2 : 10 + i * 2] + x_in[16 + i * 2 : 18 + i * 2]
        if i:
            start(across_rows.at[mine], zh_in.at[pl.ds((i - 1) * 2, 2)], s_row.at[2], r_row.at[2], peer(dzh=i))
    received(corr_in.at[pl.ds(1, 3)], r_corr.at[1])
    corr[2] = corr[1] + (corr_in[1] + corr_in[2] + corr_in[3])
    for i in (1, 2, 3):
        start(corr.at[2], corr_in.at[3 + i], s_corr.at[2], r_corr.at[2], peer(dzh=i))

    received(y_in, r_col.at[0])
    for i in (3, 2, 1, 0):
        mine = pl.ds(i * 2, 2)
        down_rows[mine] += y_in[i * 2 : i * 2 + 2] + y_in[8 + i * 2 : 10 + i * 2] + y_in[16 + i * 2 : 18 + i * 2]
        if i:
            start(down_rows.at[mine], zl_in.at[pl.ds((i - 1) * 2, 2)], s_col.at[1], r_col.at[1], peer(dzl=i))

    received(z_small, r_small.at[0])
    gram[1] = gram[0] + jnp.sum(z_small[...], axis=0)
    for n in (20, 21, 4, 5, 16, 17, 12, 13, 18, 19, 22, 23, 28, 29, 2, 3, 6, 7, 8, 9, 24, 25, 10, 11, 14, 15, 26, 27, 30, 31, 1):
        to = peer(dx=n // 8, dy=(n // 2) % 4, dc=n % 2)
        start(gram.at[1], xy_small.at[n - 1], s_small.at[1], r_small.at[1], to)

    scale = 1.0 / (1024 * TL)
    received(zl_in, r_col.at[1])
    received(zh_in, r_row.at[2])
    for b in range(2):
        images_ref[:, b * TL : (b + 1) * TL] = (
            (down_rows[b] + across_rows[b])
            + ((zl_in[b] + zl_in[2 + b] + zl_in[4 + b]) + (zh_in[b] + zh_in[2 + b] + zh_in[4 + b]))
        )
    received(corr_in.at[pl.ds(4, 3)], r_corr.at[2])
    small_ref[1] = unfold_small((corr[2] + (corr_in[4] + corr_in[5] + corr_in[6])) * scale)[0]

    for d in [far_up, far_dn, far_two, core_rs, corr_core] + near_zl:
        d.wait_send()
    left(near.at[pl.ds(0, 24)], s_near.at[0])
    left(far.at[pl.ds(0, 42)], s_far_x.at[0])
    left(far.at[pl.ds(0, 14)], s_far_x.at[1])
    left(x_in, s_row.at[1])
    left(zh_in, s_row.at[2])
    left(y_in, s_col.at[0])
    left(zl_in, s_col.at[1])
    left(corr_in.at[pl.ds(1, 3)], s_corr.at[1])
    left(corr_in.at[pl.ds(4, 3)], s_corr.at[2])
    left(z_small, s_small.at[0])
    received(xy_small, r_small.at[1])
    straight, turned = unfold_small((gram[1] + jnp.sum(xy_small[...], axis=0)) * scale)
    small_ref[0] = straight + turned
    left(xy_small, s_small.at[1])


def on_device(x_block, p_block, tile_values, tile_brow, tile_bcol, tile_count):
    slots = tile_values.shape[0]
    vmem = pl.BlockSpec(memory_space=pltpu.VMEM)
    dma = pltpu.SemaphoreType.DMA
    return pl.pallas_call(
        functools.partial(kernel, slots),
        out_shape=(
            jax.ShapeDtypeStruct((VB, 2 * TL), F32),
            jax.ShapeDtypeStruct((2, VB, VB), F32),
        ),
        in_specs=[pl.BlockSpec(memory_space=pltpu.HBM)] * 5 + [pl.BlockSpec(memory_space=pltpu.SMEM)],
        out_specs=(vmem, vmem),
        scratch_shapes=[
            pltpu.VMEM((8, 2 * TL), BF16),
            pltpu.VMEM((8, 2 * TL), BF16),
            pltpu.SMEM((slots,), jnp.int32),
            pltpu.SMEM((slots,), jnp.int32),
            pltpu.VMEM((1, slots), jnp.int32),
            pltpu.VMEM((1, slots), jnp.int32),
            pltpu.VMEM((slots, TL, TL), BF16),
            pltpu.VMEM((32, VB, TL), BF16),
            pltpu.VMEM((64, VB, TL), BF16),
            pltpu.VMEM((32 * VB, slots * VB), BF16),
            pltpu.VMEM((64 * VB, slots * VB), BF16),
            pltpu.VMEM((slots * VB, 2 * TL), BF16),
            pltpu.VMEM((32, VB, TL), F32),
            pltpu.VMEM((64, VB, TL), F32),
            pltpu.VMEM((32, VB, TL), F32),
            pltpu.VMEM((24, VB, TL), F32),
            pltpu.VMEM((6, VB, TL), F32),
            pltpu.VMEM((24, VB, TL), F32),
            pltpu.VMEM((6, VB, TL), F32),
            pltpu.VMEM((2, 2, TL), F32),
            pltpu.VMEM((15, 2, TL), F32),
            pltpu.VMEM((31, 2, TL), F32),
            pltpu.VMEM((3, 2, TL), F32),
            pltpu.VMEM((7, 2, TL), F32),
            dma((7,)),
            dma((4,)),
            dma((4,)),
            dma((3,)),
            dma((3,)),
            dma((2,)),
            dma((2,)),
            dma((3,)),
            dma((3,)),
            dma((2,)),
            dma((2,)),
            dma((2,)),
            dma((2,)),
            dma((3,)),
            dma((3,)),
        ],
        compiler_params=pltpu.CompilerParams(
            collective_id=0, has_side_effects=True, vmem_limit_bytes=32 * 2**20
        ),
    )(
        *(
            pltpu.with_memory_space_constraint(arg, pltpu.HBM)
            for arg in (
                x_block,
                p_block,
                tile_values,
                tile_brow.reshape(1, slots),
                tile_bcol.reshape(1, slots),
            )
        ),
        tile_count,
    )


def solution(mesh):
    return jax.shard_map(
        on_device,
        mesh=mesh,
        in_specs=(
            P(None, ("row", "col")),
            P(None, ("row", "col")),
            P(("row", "col"), None, None),
            P(("row", "col")),
            P(("row", "col")),
            P(("row", "col")),
        ),
        out_specs=(P(None, ("row", "col")), P()),
        check_vma=False,
    )
```

```python
import functools

import jax
import jax.numpy as jnp
from jax import lax
from jax.experimental import pallas as pl
from jax.experimental.pallas import tpu as pltpu
from jax.sharding import PartitionSpec as P

MESH = pl.DeviceIdType.MESH
F32 = jnp.float32
BF16 = jnp.bfloat16
VB = 16
TL = 128
NT = (((1,), (1,)), ((), ()))
NN = (((1,), (0,)), ((), ()))


def iota(shape, dim):
    return lax.broadcasted_iota(jnp.int32, shape, dim)


def wide_mask():
    return iota((VB, TL), 1) // VB == iota((VB, TL), 0) % 8


def eight(block):
    return jnp.concatenate([block] * 8, axis=0)


def fold_small(ref, slot, wide):
    wide = jnp.where(wide_mask(), wide, 0.0)
    ref[slot, 0:1] = jnp.sum(wide[0:8], axis=0, keepdims=True)
    ref[slot, 1:2] = jnp.sum(wide[8:16], axis=0, keepdims=True)


def unfold_small(rows):
    upper = iota((VB, TL), 0) < 8
    wide = jnp.where(upper, jnp.broadcast_to(rows[0:1], (VB, TL)), jnp.broadcast_to(rows[1:2], (VB, TL)))
    wide = jnp.where(wide_mask(), wide, 0.0)
    turned = jnp.sum(wide.T.reshape(8, VB, VB), axis=0)
    for shift in (64, 32, 16):
        wide = wide + pltpu.roll(wide, shift, 1)
    return wide[:, 0:VB], turned


def kernel(
    slots,
    x_hbm,
    p_hbm,
    tiles_hbm,
    brow_hbm,
    bcol_hbm,
    count_s,
    images_ref,
    small_ref,
    x_ref,
    p_ref,
    brow_s,
    bcol_s,
    brow_v,
    bcol_v,
    tiles,
    near,
    far,
    kron_row,
    kron_col,
    pieces,
    down_rows,
    across_rows,
    core_in,
    x_in,
    zh_in,
    y_in,
    zl_in,
    gram,
    z_small,
    xy_small,
    corr,
    corr_in,
    load_sem,
    s_near,
    r_near,
    s_far,
    r_far,
    s_far_x,
    r_far_x,
    s_row,
    r_row,
    s_col,
    r_col,
    s_small,
    r_small,
    s_corr,
    r_corr,
):
    row, col = lax.axis_index("row"), lax.axis_index("col")
    x, zh, core = row // 8, (row // 2) % 4, row % 2
    y, zl = col // 4, col % 4

    def peer(dx=0, dy=0, dzh=0, dzl=0, dc=0):
        return (
            ((x + dx) % 4) * 8 + ((zh + dzh) % 4) * 2 + (core + dc) % 2,
            ((y + dy) % 4) * 4 + (zl + dzl) % 4,
        )

    def copy(src, dst, send, recv, to):
        return pltpu.make_async_remote_copy(
            src_ref=src, dst_ref=dst, send_sem=send, recv_sem=recv, device_id=to, device_id_type=MESH
        )

    def start(src, dst, send, recv, to):
        desc = copy(src, dst, send, recv, to)
        desc.start()
        return desc

    def received(region, sem):
        copy(region, region, sem, sem, peer(dc=1)).wait_recv()

    def left(region, sem):
        copy(region, region, sem, sem, peer(dc=1)).wait_send()

    barrier = pltpu.get_barrier_semaphore()
    friends = (
        [peer(dzh=1), peer(dzh=3)]
        + [peer(dzl=i) for i in (3, 1, 2)]
        + [peer(dy=i) for i in (2, 1, 3)]
        + [peer(dx=i, dc=dc) for i in (2, 1, 3) for dc in (0, 1)]
        + [peer(dc=1)]
    )
    for to in friends:
        pl.semaphore_signal(barrier, inc=1, device_id=to, device_id_type=MESH)

    fetches = [
        pltpu.make_async_copy(src, dst, load_sem.at[n])
        for n, (src, dst) in enumerate(
            [
                (x_hbm, x_ref),
                (p_hbm, p_ref),
                (bcol_hbm, bcol_v),
                (brow_hbm, brow_v),
                (bcol_hbm.at[0], bcol_s),
                (brow_hbm.at[0], brow_s),
                (tiles_hbm, tiles),
            ]
        )
    ]
    for fetch in fetches:
        fetch.start()
    fetches[0].wait()
    fetches[1].wait()

    for b in range(2):
        own = jnp.concatenate(
            [x_ref[:, b * TL : (b + 1) * TL].astype(F32), p_ref[:, b * TL : (b + 1) * TL].astype(F32)],
            axis=0,
        ).astype(BF16)
        near[b] = own
        far[b] = own

    pl.semaphore_wait(barrier, len(friends))
    def far_spread(slot):
        block = far.at[pl.ds(slot * 2, 2)]
        for n in (2, 6, 1, 3, 5, 7, 4):
            i, dc = n % 4, n // 4
            place = pl.ds(dc * 32 + (4 - i) % 4 * 8 + slot * 2, 2)
            start(block, far.at[place], s_far_x.at[0], r_far_x.at[0], peer(dx=i, dc=dc))

    far_up = start(far.at[pl.ds(0, 2)], far.at[pl.ds(6, 2)], s_far.at[0], r_far.at[0], peer(dzh=1))
    far_dn = start(far.at[pl.ds(0, 2)], far.at[pl.ds(2, 2)], s_far.at[1], r_far.at[1], peer(dzh=3))
    near_zl = []
    for i in (3, 2, 1):
        near_zl.append(
            start(near.at[pl.ds(0, 2)], near.at[pl.ds((4 - i) * 2, 2)], s_near.at[i], r_near.at[i], peer(dzl=i))
        )

    def near_spread(slot):
        for i in (2, 1, 3):
            place = pl.ds((4 - i) * 8 + slot * 2, 2)
            start(near.at[pl.ds(slot * 2, 2)], near.at[place], s_near.at[0], r_near.at[0], peer(dy=i))

    near_spread(0)
    far_spread(0)

    def place(rel):
        lane = iota((8, slots), 1)
        rel = jnp.where(lane < count_s[0], jnp.broadcast_to(rel, (8, slots)), 255)
        spread = (iota((slots, slots * VB), 1) // VB == iota((slots, slots * VB), 0)).astype(BF16)
        wide = lax.dot_general(rel.astype(F32).astype(BF16), spread, NN, preferred_element_type=F32)
        wide = jnp.concatenate([wide, wide], axis=0)
        diag = iota((VB, slots * VB), 1) % VB == iota((VB, slots * VB), 0)
        return jnp.where(diag, wide, 255.0)

    def near_index(brow):
        c = (brow // 2) % 16
        return (((c // 4 - y) & 3) * 4 + ((c % 4 - zl) & 3)) * 2 + brow % 2

    def far_index(bcol):
        m = bcol // 32
        return (
            ((((m % 2) ^ core) * 4 + ((m // 8 - x) & 3)) * 4 + (((m // 2) % 4 - zh) & 3)) * 2 + bcol % 2
        )

    def build(ref, rel, blocks):
        placed = place(rel)

        @pl.loop(0, blocks // 8)
        def _(step):
            for j in range(8):
                b = step * 8 + j
                ref[pl.ds(pl.multiple_of(b * VB, VB), VB), :] = jnp.where(
                    placed == b.astype(F32), 1.0, 0.0
                ).astype(BF16)

    for fetch in fetches[2:6]:
        fetch.wait()
    build(kron_col, far_index(bcol_v[...]), 64)
    for j in range(3):
        i = jnp.where(zl == 0, 3 - j, 1 + j)
        received(near.at[pl.ds(0, 2)], r_near.at[i])
        near_spread(4 - i)
    far_up.wait_recv()
    far_dn.wait_recv()
    for i in (2, 1, 3, 0):
        spot = (4 - i) % 4 * 8 + 4
        start(far.at[pl.ds(6, 1)], far.at[pl.ds(spot, 1)], s_far_x.at[1], r_far_x.at[1], peer(dx=i, dzh=1))
    for i in (2, 1, 3, 0):
        spot = (4 - i) % 4 * 8 + 5
        start(far.at[pl.ds(3, 1)], far.at[pl.ds(spot, 1)], s_far_x.at[1], r_far_x.at[1], peer(dx=i, dzh=3))
    far_spread(3)
    far_spread(1)
    build(kron_row, near_index(brow_v[...]), 32)
    fetches[6].wait()
    received(near.at[pl.ds(8, 24)], r_near.at[0])

    def multiply(vec_ref, index_of, index_s, dims):
        for k in range(slots):
            part = lax.dot_general(vec_ref[index_of(index_s[k])], tiles[k], dims, preferred_element_type=F32)
            high = part.astype(BF16)
            rows = slice(k * VB, (k + 1) * VB)
            pieces[rows, 0:TL] = high
            pieces[rows, TL : 2 * TL] = (part - high.astype(F32)).astype(BF16)

    def scatter(kron, first, blocks, out_ref):
        both = lax.dot_general(
            kron[first * VB : (first + blocks) * VB, :], pieces[...], NN, preferred_element_type=F32
        )
        out_ref[first : first + blocks] = (both[:, 0:TL] + both[:, TL : 2 * TL]).reshape(blocks, VB, TL)

    multiply(near, near_index, brow_s, NN)
    scatter(kron_col, 32, 32, across_rows)
    core_rs = start(across_rows.at[pl.ds(32, 32)], core_in, s_row.at[0], r_row.at[0], peer(dc=1))
    scatter(kron_col, 0, 32, across_rows)
    core_rs.wait_recv()
    across_rows[0:32] += core_in[...]
    for first, size, group in ((4, 2, 3), (0, 4, 1), (6, 2, 1)):
        for i in (2, 1, 3):
            mine, there = pl.ds(i * 8 + first, size), pl.ds((i - 1) * 8 + first, size)
            start(across_rows.at[mine], x_in.at[there], s_row.at[group], r_row.at[group], peer(dx=i))

    def share(blocks):
        high = [across_rows[b].astype(BF16) for b in blocks]
        low = [(across_rows[b] - h.astype(F32)).astype(BF16) for b, h in zip(blocks, high)]
        both = jnp.concatenate([jnp.concatenate(part, axis=1) for part in (high, low)], axis=0)
        vecs = jnp.concatenate([eight(far[b]) for b in blocks], axis=1)
        both = lax.dot_general(both, vecs, NT, preferred_element_type=F32)
        return both[0:VB] + both[VB : 2 * VB]

    wide = jnp.concatenate([near[b] for b in range(32)], axis=1)
    tall = jnp.concatenate([eight(near[b]) for b in range(32)], axis=1)
    fold_small(corr, 0, lax.dot_general(wide, tall, NT, preferred_element_type=F32))
    corr_core = start(corr.at[0], corr_in.at[0], s_corr.at[0], r_corr.at[0], peer(dc=1))
    received(far.at[pl.ds(0, 42)], r_far_x.at[0])
    half = share([b for b in range(32) if b % 8 // 2 != 2])
    received(far.at[pl.ds(0, 8)], r_far_x.at[1])
    for i in range(4):
        block = far.at[pl.ds(i * 8 + 4, 2)]
        start(block, far.at[pl.ds(32 + i * 8 + 4, 2)], s_far.at[2], r_far.at[2], peer(dc=1))
    half = half + share([b for b in range(32) if b % 8 // 2 == 2])
    fold_small(gram, 0, half)
    for n in (8, 7, 9, 6, 10, 5, 11, 4, 12, 3, 13, 2, 14, 1, 15):
        zz = zh * 4 + zl + n
        to = (x * 8 + ((zz // 4) % 4) * 2 + core, y * 4 + zz % 4)
        start(gram.at[0], z_small.at[n - 1], s_small.at[0], r_small.at[0], to)

    corr_core.wait_recv()
    corr[1] = corr[0] + corr_in[0]
    for i in (1, 2, 3):
        start(corr.at[1], corr_in.at[i], s_corr.at[1], r_corr.at[1], peer(dx=i))
    received(far.at[pl.ds(0, 8)], r_far.at[2])
    multiply(far, far_index, bcol_s, NT)
    scatter(kron_row, 8, 24, down_rows)
    for first, size, group in ((2, 6, 0), (0, 2, 2)):
        for i in (2, 1, 3):
            mine, there = pl.ds(i * 8 + first, size), pl.ds((i - 1) * 8 + first, size)
            start(down_rows.at[mine], y_in.at[there], s_col.at[group], r_col.at[group], peer(dy=i))
    scatter(kron_row, 0, 8, down_rows)
    received(x_in.at[pl.ds(0, 6)], r_row.at[3])
    for i in (2, 1, 3, 0):
        if i == 1:
            received(x_in.at[pl.ds(0, 18)], r_row.at[1])
        mine = pl.ds(i * 2, 2)
        across_rows[mine] += x_in[i * 2 : i * 2 + 2] + x_in[8 + i * 2 : 10 + i * 2] + x_in[16 + i * 2 : 18 + i * 2]
        if i:
            start(across_rows.at[mine], zh_in.at[pl.ds((i - 1) * 2, 2)], s_row.at[2], r_row.at[2], peer(dzh=i))
    received(corr_in.at[pl.ds(1, 3)], r_corr.at[1])
    corr[2] = corr[1] + (corr_in[1] + corr_in[2] + corr_in[3])
    for i in (1, 2, 3):
        start(corr.at[2], corr_in.at[3 + i], s_corr.at[2], r_corr.at[2], peer(dzh=i))

    received(y_in.at[pl.ds(0, 18)], r_col.at[0])
    for i in (3, 2, 1, 0):
        if i == 0:
            received(y_in.at[pl.ds(0, 6)], r_col.at[2])
        mine = pl.ds(i * 2, 2)
        down_rows[mine] += y_in[i * 2 : i * 2 + 2] + y_in[8 + i * 2 : 10 + i * 2] + y_in[16 + i * 2 : 18 + i * 2]
        if i:
            start(down_rows.at[mine], zl_in.at[pl.ds((i - 1) * 2, 2)], s_col.at[1], r_col.at[1], peer(dzl=i))

    received(z_small, r_small.at[0])
    gram[1] = gram[0] + jnp.sum(z_small[...], axis=0)
    for n in (20, 21, 4, 5, 16, 17, 12, 13, 18, 19, 22, 23, 28, 29, 2, 3, 6, 7, 8, 9, 24, 25, 10, 11, 14, 15, 26, 27, 30, 31, 1):
        to = peer(dx=n // 8, dy=(n // 2) % 4, dc=n % 2)
        start(gram.at[1], xy_small.at[n - 1], s_small.at[1], r_small.at[1], to)

    scale = 1.0 / (1024 * TL)
    received(zl_in, r_col.at[1])
    received(zh_in, r_row.at[2])
    for b in range(2):
        images_ref[:, b * TL : (b + 1) * TL] = (
            (down_rows[b] + across_rows[b])
            + ((zl_in[b] + zl_in[2 + b] + zl_in[4 + b]) + (zh_in[b] + zh_in[2 + b] + zh_in[4 + b]))
        )
    received(corr_in.at[pl.ds(4, 3)], r_corr.at[2])
    small_ref[1] = unfold_small((corr[2] + (corr_in[4] + corr_in[5] + corr_in[6])) * scale)[0]

    for d in [far_up, far_dn, core_rs, corr_core] + near_zl:
        d.wait_send()
    left(near.at[pl.ds(0, 24)], s_near.at[0])
    left(far.at[pl.ds(0, 42)], s_far_x.at[0])
    left(far.at[pl.ds(0, 8)], s_far_x.at[1])
    left(far.at[pl.ds(0, 8)], s_far.at[2])
    left(x_in.at[pl.ds(0, 18)], s_row.at[1])
    left(x_in.at[pl.ds(0, 6)], s_row.at[3])
    left(zh_in, s_row.at[2])
    left(y_in.at[pl.ds(0, 18)], s_col.at[0])
    left(y_in.at[pl.ds(0, 6)], s_col.at[2])
    left(zl_in, s_col.at[1])
    left(corr_in.at[pl.ds(1, 3)], s_corr.at[1])
    left(corr_in.at[pl.ds(4, 3)], s_corr.at[2])
    left(z_small, s_small.at[0])
    received(xy_small, r_small.at[1])
    straight, turned = unfold_small((gram[1] + jnp.sum(xy_small[...], axis=0)) * scale)
    small_ref[0] = straight + turned
    left(xy_small, s_small.at[1])


def on_device(x_block, p_block, tile_values, tile_brow, tile_bcol, tile_count):
    slots = tile_values.shape[0]
    vmem = pl.BlockSpec(memory_space=pltpu.VMEM)
    dma = pltpu.SemaphoreType.DMA
    return pl.pallas_call(
        functools.partial(kernel, slots),
        out_shape=(
            jax.ShapeDtypeStruct((VB, 2 * TL), F32),
            jax.ShapeDtypeStruct((2, VB, VB), F32),
        ),
        in_specs=[pl.BlockSpec(memory_space=pltpu.HBM)] * 5 + [pl.BlockSpec(memory_space=pltpu.SMEM)],
        out_specs=(vmem, vmem),
        scratch_shapes=[
            pltpu.VMEM((8, 2 * TL), BF16),
            pltpu.VMEM((8, 2 * TL), BF16),
            pltpu.SMEM((slots,), jnp.int32),
            pltpu.SMEM((slots,), jnp.int32),
            pltpu.VMEM((1, slots), jnp.int32),
            pltpu.VMEM((1, slots), jnp.int32),
            pltpu.VMEM((slots, TL, TL), BF16),
            pltpu.VMEM((32, VB, TL), BF16),
            pltpu.VMEM((64, VB, TL), BF16),
            pltpu.VMEM((32 * VB, slots * VB), BF16),
            pltpu.VMEM((64 * VB, slots * VB), BF16),
            pltpu.VMEM((slots * VB, 2 * TL), BF16),
            pltpu.VMEM((32, VB, TL), F32),
            pltpu.VMEM((64, VB, TL), F32),
            pltpu.VMEM((32, VB, TL), F32),
            pltpu.VMEM((24, VB, TL), F32),
            pltpu.VMEM((6, VB, TL), F32),
            pltpu.VMEM((24, VB, TL), F32),
            pltpu.VMEM((6, VB, TL), F32),
            pltpu.VMEM((2, 2, TL), F32),
            pltpu.VMEM((15, 2, TL), F32),
            pltpu.VMEM((31, 2, TL), F32),
            pltpu.VMEM((3, 2, TL), F32),
            pltpu.VMEM((7, 2, TL), F32),
            dma((7,)),
            dma((4,)),
            dma((4,)),
            dma((3,)),
            dma((3,)),
            dma((2,)),
            dma((2,)),
            dma((4,)),
            dma((4,)),
            dma((3,)),
            dma((3,)),
            dma((2,)),
            dma((2,)),
            dma((3,)),
            dma((3,)),
        ],
        compiler_params=pltpu.CompilerParams(
            collective_id=0, has_side_effects=True, vmem_limit_bytes=32 * 2**20
        ),
    )(
        *(
            pltpu.with_memory_space_constraint(arg, pltpu.HBM)
            for arg in (
                x_block,
                p_block,
                tile_values,
                tile_brow.reshape(1, slots),
                tile_bcol.reshape(1, slots),
            )
        ),
        tile_count,
    )


def solution(mesh):
    return jax.shard_map(
        on_device,
        mesh=mesh,
        in_specs=(
            P(None, ("row", "col")),
            P(None, ("row", "col")),
            P(("row", "col"), None, None),
            P(("row", "col")),
            P(("row", "col")),
            P(("row", "col")),
        ),
        out_specs=(P(None, ("row", "col")), P()),
        check_vma=False,
    )
```

```python
import functools

import jax
import jax.numpy as jnp
from jax import lax
from jax.experimental import pallas as pl
from jax.experimental.pallas import tpu as pltpu
from jax.sharding import PartitionSpec as P

MESH = pl.DeviceIdType.MESH
F32 = jnp.float32
BF16 = jnp.bfloat16
VB = 16
TL = 128
NT = (((1,), (1,)), ((), ()))
NN = (((1,), (0,)), ((), ()))


def iota(shape, dim):
    return lax.broadcasted_iota(jnp.int32, shape, dim)


def wide_mask():
    return iota((VB, TL), 1) // VB == iota((VB, TL), 0) % 8


def eight(block):
    return jnp.concatenate([block] * 8, axis=0)


def fold_small(ref, slot, wide):
    wide = jnp.where(wide_mask(), wide, 0.0)
    ref[slot, 0:1] = jnp.sum(wide[0:8], axis=0, keepdims=True)
    ref[slot, 1:2] = jnp.sum(wide[8:16], axis=0, keepdims=True)


def unfold_small(rows):
    upper = iota((VB, TL), 0) < 8
    wide = jnp.where(upper, jnp.broadcast_to(rows[0:1], (VB, TL)), jnp.broadcast_to(rows[1:2], (VB, TL)))
    wide = jnp.where(wide_mask(), wide, 0.0)
    turned = jnp.sum(wide.T.reshape(8, VB, VB), axis=0)
    for shift in (64, 32, 16):
        wide = wide + pltpu.roll(wide, shift, 1)
    return wide[:, 0:VB], turned


def kernel(
    slots,
    x_hbm,
    p_hbm,
    tiles_hbm,
    brow_hbm,
    bcol_hbm,
    count_s,
    images_ref,
    small_ref,
    x_ref,
    p_ref,
    brow_s,
    bcol_s,
    brow_v,
    bcol_v,
    tiles,
    near,
    far,
    kron_row,
    kron_col,
    pieces,
    down_rows,
    across_rows,
    core_in,
    x_in,
    zh_in,
    y_in,
    zl_in,
    gram,
    z_small,
    xy_small,
    corr,
    corr_in,
    load_sem,
    s_near,
    r_near,
    s_far,
    r_far,
    s_far_x,
    r_far_x,
    s_row,
    r_row,
    s_col,
    r_col,
    s_small,
    r_small,
    s_corr,
    r_corr,
):
    row, col = lax.axis_index("row"), lax.axis_index("col")
    x, zh, core = row // 8, (row // 2) % 4, row % 2
    y, zl = col // 4, col % 4

    def peer(dx=0, dy=0, dzh=0, dzl=0, dc=0):
        return (
            ((x + dx) % 4) * 8 + ((zh + dzh) % 4) * 2 + (core + dc) % 2,
            ((y + dy) % 4) * 4 + (zl + dzl) % 4,
        )

    def copy(src, dst, send, recv, to):
        return pltpu.make_async_remote_copy(
            src_ref=src, dst_ref=dst, send_sem=send, recv_sem=recv, device_id=to, device_id_type=MESH
        )

    def start(src, dst, send, recv, to):
        desc = copy(src, dst, send, recv, to)
        desc.start()
        return desc

    def received(region, sem):
        copy(region, region, sem, sem, peer(dc=1)).wait_recv()

    def left(region, sem):
        copy(region, region, sem, sem, peer(dc=1)).wait_send()

    barrier = pltpu.get_barrier_semaphore()
    friends = (
        [peer(dzh=1), peer(dzh=3)]
        + [peer(dzl=i) for i in (3, 1, 2)]
        + [peer(dy=i) for i in (2, 1, 3)]
        + [peer(dx=i, dc=dc) for i in (2, 1, 3) for dc in (0, 1)]
        + [peer(dc=1)]
    )
    for to in friends:
        pl.semaphore_signal(barrier, inc=1, device_id=to, device_id_type=MESH)

    fetches = [
        pltpu.make_async_copy(src, dst, load_sem.at[n])
        for n, (src, dst) in enumerate(
            [
                (x_hbm, x_ref),
                (p_hbm, p_ref),
                (bcol_hbm, bcol_v),
                (brow_hbm, brow_v),
                (bcol_hbm.at[0], bcol_s),
                (brow_hbm.at[0], brow_s),
                (tiles_hbm, tiles),
            ]
        )
    ]
    for fetch in fetches:
        fetch.start()
    fetches[0].wait()
    fetches[1].wait()

    for b in range(2):
        own = jnp.concatenate(
            [x_ref[:, b * TL : (b + 1) * TL].astype(F32), p_ref[:, b * TL : (b + 1) * TL].astype(F32)],
            axis=0,
        ).astype(BF16)
        near[b] = own
        far[b] = own

    pl.semaphore_wait(barrier, len(friends))
    def far_spread(slot):
        block = far.at[pl.ds(slot * 2, 2)]
        for n in (2, 6, 1, 3, 5, 7, 4):
            i, dc = n % 4, n // 4
            place = pl.ds(dc * 32 + (4 - i) % 4 * 8 + slot * 2, 2)
            start(block, far.at[place], s_far_x.at[0], r_far_x.at[0], peer(dx=i, dc=dc))

    far_up = start(far.at[pl.ds(0, 2)], far.at[pl.ds(6, 2)], s_far.at[0], r_far.at[0], peer(dzh=1))
    far_dn = start(far.at[pl.ds(0, 2)], far.at[pl.ds(2, 2)], s_far.at[1], r_far.at[1], peer(dzh=3))
    near_zl = []
    for i in (3, 2, 1):
        near_zl.append(
            start(near.at[pl.ds(0, 2)], near.at[pl.ds((4 - i) * 2, 2)], s_near.at[i], r_near.at[i], peer(dzl=i))
        )

    def near_spread(slot):
        for i in (2, 1, 3):
            place = pl.ds((4 - i) * 8 + slot * 2, 2)
            start(near.at[pl.ds(slot * 2, 2)], near.at[place], s_near.at[0], r_near.at[0], peer(dy=i))

    near_spread(0)
    far_spread(0)

    def place(rel):
        lane = iota((8, slots), 1)
        rel = jnp.where(lane < count_s[0], jnp.broadcast_to(rel, (8, slots)), 255)
        spread = (iota((slots, slots * VB), 1) // VB == iota((slots, slots * VB), 0)).astype(BF16)
        wide = lax.dot_general(rel.astype(F32).astype(BF16), spread, NN, preferred_element_type=F32)
        wide = jnp.concatenate([wide, wide], axis=0)
        diag = iota((VB, slots * VB), 1) % VB == iota((VB, slots * VB), 0)
        return jnp.where(diag, wide, 255.0)

    def near_index(brow):
        c = (brow // 2) % 16
        return (((c // 4 - y) & 3) * 4 + ((c % 4 - zl) & 3)) * 2 + brow % 2

    def far_index(bcol):
        m = bcol // 32
        return (
            ((((m % 2) ^ core) * 4 + ((m // 8 - x) & 3)) * 4 + (((m // 2) % 4 - zh) & 3)) * 2 + bcol % 2
        )

    def build(ref, rel, blocks):
        placed = place(rel)

        @pl.loop(0, blocks // 8)
        def _(step):
            for j in range(8):
                b = step * 8 + j
                ref[pl.ds(pl.multiple_of(b * VB, VB), VB), :] = jnp.where(
                    placed == b.astype(F32), 1.0, 0.0
                ).astype(BF16)

    for fetch in fetches[2:6]:
        fetch.wait()
    build(kron_col, far_index(bcol_v[...]), 64)
    for j in range(3):
        i = jnp.where(zl == 0, 3 - j, 1 + j)
        received(near.at[pl.ds(0, 2)], r_near.at[i])
        near_spread(4 - i)
    far_up.wait_recv()
    far_dn.wait_recv()
    for i in (2, 1, 3, 0):
        spot = (4 - i) % 4 * 8 + 4
        start(far.at[pl.ds(6, 1)], far.at[pl.ds(spot, 1)], s_far_x.at[1], r_far_x.at[1], peer(dx=i, dzh=1))
    for i in (2, 1, 3, 0):
        spot = (4 - i) % 4 * 8 + 5
        start(far.at[pl.ds(3, 1)], far.at[pl.ds(spot, 1)], s_far_x.at[1], r_far_x.at[1], peer(dx=i, dzh=3))
    far_spread(3)
    far_spread(1)
    build(kron_row, near_index(brow_v[...]), 32)
    fetches[6].wait()
    received(near.at[pl.ds(8, 24)], r_near.at[0])

    def multiply(vec_ref, index_of, index_s, dims):
        for k in range(slots):
            part = lax.dot_general(vec_ref[index_of(index_s[k])], tiles[k], dims, preferred_element_type=F32)
            high = part.astype(BF16)
            rows = slice(k * VB, (k + 1) * VB)
            pieces[rows, 0:TL] = high
            pieces[rows, TL : 2 * TL] = (part - high.astype(F32)).astype(BF16)

    def scatter(kron, first, blocks, out_ref):
        both = lax.dot_general(
            kron[first * VB : (first + blocks) * VB, :], pieces[...], NN, preferred_element_type=F32
        )
        out_ref[first : first + blocks] = (both[:, 0:TL] + both[:, TL : 2 * TL]).reshape(blocks, VB, TL)

    multiply(near, near_index, brow_s, NN)
    scatter(kron_col, 32, 32, across_rows)
    core_rs = start(across_rows.at[pl.ds(32, 32)], core_in, s_row.at[0], r_row.at[0], peer(dc=1))
    scatter(kron_col, 0, 32, across_rows)
    wide = jnp.concatenate([near[b] for b in range(32)], axis=1)
    tall = jnp.concatenate([eight(near[b]) for b in range(32)], axis=1)
    fold_small(corr, 0, lax.dot_general(wide, tall, NT, preferred_element_type=F32))
    corr_core = start(corr.at[0], corr_in.at[0], s_corr.at[0], r_corr.at[0], peer(dc=1))
    core_rs.wait_recv()
    across_rows[0:32] += core_in[...]
    for first, size, group in ((4, 2, 3), (0, 4, 1), (6, 2, 1)):
        for i in (2, 1, 3):
            mine, there = pl.ds(i * 8 + first, size), pl.ds((i - 1) * 8 + first, size)
            start(across_rows.at[mine], x_in.at[there], s_row.at[group], r_row.at[group], peer(dx=i))

    def share(blocks):
        high = [across_rows[b].astype(BF16) for b in blocks]
        low = [(across_rows[b] - h.astype(F32)).astype(BF16) for b, h in zip(blocks, high)]
        both = jnp.concatenate([jnp.concatenate(part, axis=1) for part in (high, low)], axis=0)
        vecs = jnp.concatenate([eight(far[b]) for b in blocks], axis=1)
        both = lax.dot_general(both, vecs, NT, preferred_element_type=F32)
        return both[0:VB] + both[VB : 2 * VB]

    received(far.at[pl.ds(0, 42)], r_far_x.at[0])
    half = share([b for b in range(32) if b % 8 // 2 != 2])
    received(far.at[pl.ds(0, 8)], r_far_x.at[1])
    for i in range(4):
        block = far.at[pl.ds(i * 8 + 4, 2)]
        start(block, far.at[pl.ds(32 + i * 8 + 4, 2)], s_far.at[2], r_far.at[2], peer(dc=1))
    half = half + share([b for b in range(32) if b % 8 // 2 == 2])
    fold_small(gram, 0, half)
    for n in (8, 7, 9, 6, 10, 5, 11, 4, 12, 3, 13, 2, 14, 1, 15):
        zz = zh * 4 + zl + n
        to = (x * 8 + ((zz // 4) % 4) * 2 + core, y * 4 + zz % 4)
        start(gram.at[0], z_small.at[n - 1], s_small.at[0], r_small.at[0], to)

    corr_core.wait_recv()
    corr[1] = corr[0] + corr_in[0]
    for i in (1, 2, 3):
        start(corr.at[1], corr_in.at[i], s_corr.at[1], r_corr.at[1], peer(dx=i))
    received(far.at[pl.ds(0, 8)], r_far.at[2])
    multiply(far, far_index, bcol_s, NT)
    scatter(kron_row, 8, 24, down_rows)
    for first, size, group in ((2, 6, 0), (0, 2, 2)):
        for i in (2, 1, 3):
            mine, there = pl.ds(i * 8 + first, size), pl.ds((i - 1) * 8 + first, size)
            start(down_rows.at[mine], y_in.at[there], s_col.at[group], r_col.at[group], peer(dy=i))
    scatter(kron_row, 0, 8, down_rows)
    received(x_in.at[pl.ds(0, 6)], r_row.at[3])
    for i in (2, 1, 3, 0):
        if i == 1:
            received(x_in.at[pl.ds(0, 18)], r_row.at[1])
        mine = pl.ds(i * 2, 2)
        across_rows[mine] += x_in[i * 2 : i * 2 + 2] + x_in[8 + i * 2 : 10 + i * 2] + x_in[16 + i * 2 : 18 + i * 2]
        if i:
            start(across_rows.at[mine], zh_in.at[pl.ds((i - 1) * 2, 2)], s_row.at[2], r_row.at[2], peer(dzh=i))
    received(corr_in.at[pl.ds(1, 3)], r_corr.at[1])
    corr[2] = corr[1] + (corr_in[1] + corr_in[2] + corr_in[3])
    for i in (1, 2, 3):
        start(corr.at[2], corr_in.at[3 + i], s_corr.at[2], r_corr.at[2], peer(dzh=i))

    received(y_in.at[pl.ds(0, 18)], r_col.at[0])
    for i in (3, 2, 1, 0):
        if i == 0:
            received(y_in.at[pl.ds(0, 6)], r_col.at[2])
        mine = pl.ds(i * 2, 2)
        down_rows[mine] += y_in[i * 2 : i * 2 + 2] + y_in[8 + i * 2 : 10 + i * 2] + y_in[16 + i * 2 : 18 + i * 2]
        if i:
            start(down_rows.at[mine], zl_in.at[pl.ds((i - 1) * 2, 2)], s_col.at[1], r_col.at[1], peer(dzl=i))

    received(z_small, r_small.at[0])
    gram[1] = gram[0] + jnp.sum(z_small[...], axis=0)
    for n in (20, 21, 4, 5, 16, 17, 12, 13, 18, 19, 22, 23, 28, 29, 2, 3, 6, 7, 8, 9, 24, 25, 10, 11, 14, 15, 26, 27, 30, 31, 1):
        to = peer(dx=n // 8, dy=(n // 2) % 4, dc=n % 2)
        start(gram.at[1], xy_small.at[n - 1], s_small.at[1], r_small.at[1], to)

    scale = 1.0 / (1024 * TL)
    received(zl_in, r_col.at[1])
    received(zh_in, r_row.at[2])
    for b in range(2):
        images_ref[:, b * TL : (b + 1) * TL] = (
            (down_rows[b] + across_rows[b])
            + ((zl_in[b] + zl_in[2 + b] + zl_in[4 + b]) + (zh_in[b] + zh_in[2 + b] + zh_in[4 + b]))
        )
    received(corr_in.at[pl.ds(4, 3)], r_corr.at[2])
    small_ref[1] = unfold_small((corr[2] + (corr_in[4] + corr_in[5] + corr_in[6])) * scale)[0]

    for d in [far_up, far_dn, core_rs, corr_core] + near_zl:
        d.wait_send()
    left(near.at[pl.ds(0, 24)], s_near.at[0])
    left(far.at[pl.ds(0, 42)], s_far_x.at[0])
    left(far.at[pl.ds(0, 8)], s_far_x.at[1])
    left(far.at[pl.ds(0, 8)], s_far.at[2])
    left(x_in.at[pl.ds(0, 18)], s_row.at[1])
    left(x_in.at[pl.ds(0, 6)], s_row.at[3])
    left(zh_in, s_row.at[2])
    left(y_in.at[pl.ds(0, 18)], s_col.at[0])
    left(y_in.at[pl.ds(0, 6)], s_col.at[2])
    left(zl_in, s_col.at[1])
    left(corr_in.at[pl.ds(1, 3)], s_corr.at[1])
    left(corr_in.at[pl.ds(4, 3)], s_corr.at[2])
    left(z_small, s_small.at[0])
    received(xy_small, r_small.at[1])
    straight, turned = unfold_small((gram[1] + jnp.sum(xy_small[...], axis=0)) * scale)
    small_ref[0] = straight + turned
    left(xy_small, s_small.at[1])


def on_device(x_block, p_block, tile_values, tile_brow, tile_bcol, tile_count):
    slots = tile_values.shape[0]
    vmem = pl.BlockSpec(memory_space=pltpu.VMEM)
    dma = pltpu.SemaphoreType.DMA
    return pl.pallas_call(
        functools.partial(kernel, slots),
        out_shape=(
            jax.ShapeDtypeStruct((VB, 2 * TL), F32),
            jax.ShapeDtypeStruct((2, VB, VB), F32),
        ),
        in_specs=[pl.BlockSpec(memory_space=pltpu.HBM)] * 5 + [pl.BlockSpec(memory_space=pltpu.SMEM)],
        out_specs=(vmem, vmem),
        scratch_shapes=[
            pltpu.VMEM((8, 2 * TL), BF16),
            pltpu.VMEM((8, 2 * TL), BF16),
            pltpu.SMEM((slots,), jnp.int32),
            pltpu.SMEM((slots,), jnp.int32),
            pltpu.VMEM((1, slots), jnp.int32),
            pltpu.VMEM((1, slots), jnp.int32),
            pltpu.VMEM((slots, TL, TL), BF16),
            pltpu.VMEM((32, VB, TL), BF16),
            pltpu.VMEM((64, VB, TL), BF16),
            pltpu.VMEM((32 * VB, slots * VB), BF16),
            pltpu.VMEM((64 * VB, slots * VB), BF16),
            pltpu.VMEM((slots * VB, 2 * TL), BF16),
            pltpu.VMEM((32, VB, TL), F32),
            pltpu.VMEM((64, VB, TL), F32),
            pltpu.VMEM((32, VB, TL), F32),
            pltpu.VMEM((24, VB, TL), F32),
            pltpu.VMEM((6, VB, TL), F32),
            pltpu.VMEM((24, VB, TL), F32),
            pltpu.VMEM((6, VB, TL), F32),
            pltpu.VMEM((2, 2, TL), F32),
            pltpu.VMEM((15, 2, TL), F32),
            pltpu.VMEM((31, 2, TL), F32),
            pltpu.VMEM((3, 2, TL), F32),
            pltpu.VMEM((7, 2, TL), F32),
            dma((7,)),
            dma((4,)),
            dma((4,)),
            dma((3,)),
            dma((3,)),
            dma((2,)),
            dma((2,)),
            dma((4,)),
            dma((4,)),
            dma((3,)),
            dma((3,)),
            dma((2,)),
            dma((2,)),
            dma((3,)),
            dma((3,)),
        ],
        compiler_params=pltpu.CompilerParams(
            collective_id=0, has_side_effects=True, vmem_limit_bytes=32 * 2**20
        ),
    )(
        *(
            pltpu.with_memory_space_constraint(arg, pltpu.HBM)
            for arg in (
                x_block,
                p_block,
                tile_values,
                tile_brow.reshape(1, slots),
                tile_bcol.reshape(1, slots),
            )
        ),
        tile_count,
    )


def solution(mesh):
    return jax.shard_map(
        on_device,
        mesh=mesh,
        in_specs=(
            P(None, ("row", "col")),
            P(None, ("row", "col")),
            P(("row", "col"), None, None),
            P(("row", "col")),
            P(("row", "col")),
            P(("row", "col")),
        ),
        out_specs=(P(None, ("row", "col")), P()),
        check_vma=False,
    )
```
